128 devices in a mesh: row: 8 (over z_hi, y), col: 16 (over x, z_lo, core).
Axes of the slice: x: 4, y: 4, z: 4 (z_hi: 2, z_lo: 2; z = z_hi * 2 + z_lo), core: 2. Of those that a mesh axis runs over, the one named last changes fastest.
Arguments:
- start_block: float32 [64, 65536], P(None, 'row'), may hold values from -6 to 6
- tile_values: bfloat16 [8, 16, 128, 256, 256], P('row', 'col'), may hold values from -0.03125 to 0.03125
- tile_rows: int32 [8, 16, 128], P('row', 'col'), may hold values from 0 to 31
- tile_cols: int32 [8, 16, 128], P('row', 'col'), may hold values from 0 to 15
Outputs:
- alphas: float32 [3, 64, 64], replicated
- betas: float32 [3, 64, 64], replicated
- final_basis: float32 [64, 65536], P(None, 'row')
The draws below stay inside these ranges and needn't reach their ends.
All inputs are finite; a program needn't handle non-finite values.
Results may differ from the reference program's by a relative error of at most 0.007.
Values may be sent and summed in bfloat16 or wider, within the bound.
A program may use at most 128 MiB of HBM per device.

```python
import math
import jax
import jax.numpy as jnp
from jax import lax

TILE = 256
NV = 64
ITERS = 3
K = 128
BC = 16
BR = 32
NB = 256
N = 65536
N_ROW = 8
N_COL = 16


def set_ends(result, stream_key, low, top_value):
    longest = result.shape.index(max(result.shape))
    spots = []
    for shift in (0, 1):
        where = [jax.random.randint(jax.random.fold_in(stream_key, axis), (), 0, length) for axis, length in enumerate(result.shape)]
        where[longest] = (where[longest] + shift) % result.shape[longest]
        spots.append(tuple(where))
    return result.at[spots[0]].set(low).at[spots[1]].set(top_value)


def level_of(own_key, extent, cuts, smallest, top_value):
    loudness, own = 1.0, jax.random.fold_in(own_key, 6)
    for axis_at, blocks in cuts:
        steps = jnp.exp(jax.random.uniform(jax.random.fold_in(own, axis_at), (blocks,), jnp.float32, smallest / len(cuts), top_value / len(cuts)))
        loudness = loudness * jnp.repeat(steps, extent[axis_at] // blocks).reshape([-1 if axis == axis_at else 1 for axis in range(len(extent))])
    return loudness


def scatter_about(key, dims, deviation, limit, shards=(), kind=jnp.bfloat16):
    factor_of = level_of(key, dims, shards, -0.22, 0.18) if shards else 1.0
    values = jax.random.normal(key, dims, jnp.float32) * deviation * factor_of
    return jnp.minimum(jnp.maximum(values, -limit), limit).astype(kind)


def setup_inputs(seed: int = 0) -> dict:
    streams_of = jax.random.split(jax.random.key(seed), 5)
    start_block = scatter_about(streams_of[0], (NV, N), 1.0, 6.0, ((1, 8),), jnp.float32)
    tile_values = scatter_about(streams_of[1], (N_ROW, N_COL, K, TILE, TILE), (2 * TILE * N_ROW * K // BC) ** -0.5, 0.03125, ((0, 8), (1, 16)))
    tile_rows = set_ends(jax.random.randint(streams_of[2], (N_ROW, N_COL, K), 0, BR), jax.random.fold_in(streams_of[2], 1), 0, BR - 1).astype(jnp.int32)
    tile_cols = set_ends(jax.random.randint(streams_of[3], (N_ROW, N_COL, K), 0, BC), jax.random.fold_in(streams_of[3], 1), 0, BC - 1).astype(jnp.int32)
    return {"start_block": start_block, "tile_values": tile_values, "tile_rows": tile_rows, "tile_cols": tile_cols}


HIGH = lax.Precision.HIGHEST

def apply_matrix(rounded, tile_values, tile_rows, tile_cols):
    blocks = rounded.astype(jnp.float32).reshape(NV, NB, TILE)
    cell_count = N_ROW * N_COL
    flat_tiles = tile_values.reshape(cell_count, K, TILE, TILE)
    flat_rows = tile_rows.reshape(cell_count, K)
    flat_cols = tile_cols.reshape(cell_count, K)

    def visit(running, inputs):
        cell_tiles, rows_here, cols_here, cell_index = inputs
        block_row = (cell_index // N_COL * BR + rows_here).astype(jnp.int32)
        block_col = (cell_index % N_COL * BC + cols_here).astype(jnp.int32)
        widened = cell_tiles.astype(jnp.float32)
        upper_part = jnp.einsum('kij,vkj->vki', widened, blocks[:, block_col, :], precision=HIGH)
        lower_part = jnp.einsum('kij,vki->vkj', widened, blocks[:, block_row, :], precision=HIGH)
        running = running.at[:, block_row, :].add(upper_part)
        running = running.at[:, block_col, :].add(lower_part)
        return (running, None)
    start_sum = jnp.zeros((NV, NB, TILE), jnp.float32)
    running, _ = lax.scan(visit, start_sum, (flat_tiles, flat_rows, flat_cols, jnp.arange(cell_count, dtype=jnp.int32)))
    return running.reshape(NV, NB * TILE)

def orthonormalize(block_rows):
    gram_matrix = jnp.dot(block_rows, block_rows.T, precision=HIGH)
    factor = jnp.linalg.cholesky(gram_matrix)
    solved = lax.linalg.triangular_solve(factor, block_rows, left_side=True, lower=True)
    return (solved, factor)

def reference(start_block, tile_values, tile_rows, tile_cols):
    basis, factor = orthonormalize(start_block)
    previous = jnp.zeros_like(basis)
    alpha_list = []
    beta_list = []
    for step_index in range(ITERS):
        applied = apply_matrix(basis.astype(jnp.bfloat16), tile_values, tile_rows, tile_cols)
        residual = applied - jnp.dot(factor.T, previous, precision=HIGH)
        alpha_block = jnp.dot(basis, residual.T, precision=HIGH)
        residual = residual - jnp.dot(alpha_block.T, basis, precision=HIGH)
        next_basis, factor = orthonormalize(residual)
        alpha_list.append(alpha_block)
        beta_list.append(factor.T)
        previous = basis
        basis = next_basis
    return (jnp.stack(alpha_list), jnp.stack(beta_list), basis * math.sqrt(N))
```

```python
import math

import jax
import jax.numpy as jnp
from jax import lax
from jax.experimental import pallas as pl
from jax.experimental.pallas import tpu as pltpu
from jax.sharding import PartitionSpec as P

ITERS = 3
HIGH = lax.Precision.HIGHEST
MESH = pl.DeviceIdType.MESH
F32 = jnp.float32
BF16 = jnp.bfloat16
NT = (((1,), (1,)), ((), ()))
NN = (((1,), (0,)), ((), ()))
UNROLL = 16


def dot_high(a, b, dims=NN):
    return lax.dot_general(a, b, dims, precision=HIGH, preferred_element_type=F32)


def factor_rows(rows):
    lane = lax.broadcasted_iota(jnp.int32, (8, 128), 1)
    sub = lax.broadcasted_iota(jnp.int32, (8, 128), 0)
    for j in range(64):
        at, inner = divmod(j, 8)
        pivot_row = rows[at][inner : inner + 1, :]
        inverse = 1.0 / pivot_row[:, j : j + 1]
        for i in range(at, 8):
            scale = jnp.broadcast_to(rows[i][:, j : j + 1] * inverse, (8, 128))
            if i == at:
                scale = jnp.where(sub > inner, scale, 0.0)
            rows[i] = rows[i] - scale * pivot_row
    done = []
    for i in range(8):
        diagonal = jnp.sum(jnp.where(lane == sub + 8 * i, rows[i], 0.0), axis=1, keepdims=True)
        scaled = rows[i] * lax.rsqrt(diagonal)
        done.append(jnp.where((lane < sub + 8 * i) & (lane < 64), 0.0, scaled))
    return done


def kernel(
    perm_r, col_of, keep_r, last_r, has_r, perm_c, row_of, keep_c, last_c, has_c,
    start, tiles_hbm,
    alphas, betas, final,
    tiles, slots, v_row, v_col, upper, lower, low_send,
    half_in, x_send, x_in, y_in, row_in, col_in, col_sum,
    wq, prev, fact, g_send, g_one, g_two, g_three,
    load_sem, start_sem,
    ag1_s, ag1_r, agx_s, agx_r, agy_s, agy_r, agc_s, agc_r,
    rsc_s, rsc_r, rsx_s, rsx_r, rsy_s, rsy_r, rsf_s, rsf_r,
    g1_s, g1_r, g2_s, g2_r, g3_s, g3_r,
):
    r = lax.axis_index("row")
    c = lax.axis_index("col")
    zh, y = r // 4, r % 4
    x, zl, k = c // 4, (c // 2) % 2, c % 2
    core = (r, c + 1 - 2 * k)
    pair = (r, c + 2 - 4 * zl)
    x_at = [(x + i) % 4 for i in range(4)]
    y_at = [(y + i) % 4 for i in range(4)]
    x_dev = [(r, i * 4 + zl * 2 + k) for i in x_at]
    y_dev = [(zh * 4 + i, c) for i in y_at]
    holders = [(e * 4 + x, (zh * 2 + y // 2) * 4 + (y % 2) * 2 + (1 - k)) for e in (0, 1)]
    owners = [(2 * x + zl, y * 4 + e * 2 + (1 - k)) for e in (0, 1)]
    mine = (1 - k) * 16
    other = k * 16
    home = mine + 4 * x + 2 * zl

    load = pltpu.make_async_copy(tiles_hbm, tiles, load_sem)
    load.start()
    first = pltpu.make_async_copy(
        start.at[:, pl.ds(pl.multiple_of(home * 256, 512), 512)], wq.at[pl.ds(0, 64), :], start_sem
    )
    first.start()

    barrier = pltpu.get_barrier_semaphore()

    def greet_row(i, _):
        pl.semaphore_signal(barrier, inc=1, device_id=(r, (c + i) % 16), device_id_type=MESH)
        return 0

    def greet_col(i, _):
        pl.semaphore_signal(barrier, inc=1, device_id=((r + i) % 8, c), device_id_type=MESH)
        return 0

    lax.fori_loop(1, 16, greet_row, 0)
    lax.fori_loop(1, 8, greet_col, 0)
    for device in holders + owners:
        pl.semaphore_signal(barrier, inc=1, device_id=device, device_id_type=MESH)
    wq[pl.ds(64, 64), :] = jnp.zeros((64, 512), F32)
    prev[...] = jnp.zeros_like(prev)
    first.wait()
    pl.semaphore_wait(barrier, 26)

    def remote(src, dst, s, d, device):
        return pltpu.make_async_remote_copy(
            src_ref=src, dst_ref=dst, send_sem=s, recv_sem=d, device_id=device, device_id_type=MESH
        )

    def sum_over_devices():
        gram = dot_high(wq[pl.ds(0, 64), :], wq[...], NT)
        for i in range(16):
            g_send[i] = gram[4 * i : 4 * i + 4, :]
        g_one[c] = g_send[c]

        def one(i):
            p = (c + i) % 16
            return remote(g_send.at[p], g_one.at[c], g1_s.at[i], g1_r.at[c], (r, p))

        def one_in(i):
            p = (c + i) % 16
            return remote(g_send.at[p], g_one.at[p], g1_s.at[i], g1_r.at[p], (r, p))

        def two(i):
            p = (r + i) % 8
            return remote(g_two.at[r], g_two.at[r], g2_s.at[i], g2_r.at[r], (p, c))

        def two_in(i):
            p = (r + i) % 8
            return remote(g_two.at[p], g_two.at[p], g2_s.at[i], g2_r.at[p], (p, c))

        def three(i):
            p = (c + i) % 16
            return remote(g_three.at[c], g_three.at[c], g3_s.at[i], g3_r.at[c], (r, p))

        def three_in(i):
            p = (c + i) % 16
            return remote(g_three.at[p], g_three.at[p], g3_s.at[i], g3_r.at[p], (r, p))

        def each(count, do):
            def step(i, _):
                do(i)
                return 0

            lax.fori_loop(1, count, step, 0)

        each(16, lambda i: one(i).start())
        each(16, lambda i: one_in(i).wait_recv())
        g_two[r] = jnp.sum(g_one[...], axis=0)
        each(8, lambda i: two(i).start())
        each(8, lambda i: two_in(i).wait_recv())
        g_three[c] = jnp.sum(g_two[...], axis=0)
        each(16, lambda i: three(i).start())
        each(16, lambda i: three_in(i).wait_recv())
        each(16, lambda i: one(i).wait_send())
        each(8, lambda i: two(i).wait_send())
        each(16, lambda i: three(i).wait_send())
        for i in range(16):
            fact[pl.ds(4 * i, 4), :] = g_three[i]

    def orthonormalize(keep):
        sum_over_devices()
        cross = fact[:, 64:128]
        keep(0, cross)
        fact[:, 0:64] = fact[:, 0:64] - dot_high(cross, cross, NT)
        eye_r = lax.broadcasted_iota(jnp.int32, (64, 64), 0)
        eye_c = lax.broadcasted_iota(jnp.int32, (64, 64), 1)
        fact[:, 64:128] = (eye_r == eye_c).astype(F32)
        done = factor_rows([fact[8 * i : 8 * i + 8, :] for i in range(8)])
        for i in range(8):
            fact[8 * i : 8 * i + 8, :] = done[i]
        keep(1, fact[:, 0:64])
        old = wq[pl.ds(64, 64), :]
        residual = wq[pl.ds(0, 64), :] - dot_high(cross, old)
        new = dot_high(fact[:, 64:128], residual)
        prev[...] = old
        wq[pl.ds(64, 64), :] = new
        rounded = new.astype(BF16)
        v_row[home] = rounded[:, 0:256]
        v_row[home + 1] = rounded[:, 256:512]

    def gather_x_begin():
        block = v_row.at[pl.ds(home, 2)]
        sent = [remote(block, block, ag1_s.at[0], ag1_r.at[0], pair)]
        for i in (1, 2, 3):
            sent.append(remote(block, block, agx_s.at[i, 0], agx_r.at[x, zl], x_dev[i]))
        return sent

    def gather_x_forward():
        theirs = mine + 4 * x + 2 * (1 - zl)
        block = v_row.at[pl.ds(theirs, 2)]
        remote(block, block, ag1_s.at[0], ag1_r.at[0], pair).wait_recv()
        sent = []
        for i in (1, 2, 3):
            sent.append(remote(block, block, agx_s.at[i, 1], agx_r.at[x, 1 - zl], x_dev[i]))
        whole = v_row.at[pl.ds(mine + 4 * x, 4)]
        sent.append(remote(whole, whole, agc_s.at[0], agc_r.at[x], core))
        return sent

    def gather_x_finish():
        sent = []
        for i in (1, 3, 2):
            for e in (0, 1):
                block = v_row.at[pl.ds(mine + 4 * x_at[i] + 2 * e, 2)]
                remote(block, block, agx_s.at[i, 0], agx_r.at[x_at[i], e], x_dev[i]).wait_recv()
            whole = v_row.at[pl.ds(mine + 4 * x_at[i], 4)]
            copy = remote(whole, whole, agc_s.at[i], agc_r.at[x_at[i]], core)
            copy.start()
            sent.append(copy)
        return sent

    def gather_core_wait():
        for i in range(4):
            whole = v_row.at[pl.ds(other + 4 * x_at[i], 4)]
            remote(whole, whole, agc_s.at[i], agc_r.at[x_at[i]], core).wait_recv()

    def multiply_up(low, high, running):
        def step(j, acc):
            for i in range(UNROLL):
                p = j * UNROLL + i
                part = lax.dot_general(
                    v_col[col_of[p]], tiles[perm_r[p]], NT, preferred_element_type=F32
                )
                acc = acc * keep_r[p] + part
                slots[p] = acc
            return acc

        return lax.fori_loop(low, high, step, running)

    def multiply_down(low, high, running):
        def step(j, acc):
            for i in range(UNROLL):
                p = j * UNROLL + i
                part = lax.dot_general(
                    v_row[row_of[p]], tiles[perm_c[p]], NN, preferred_element_type=F32
                )
                acc = acc * keep_c[p] + part
                slots[p] = acc
            return acc

        return lax.fori_loop(low, high, step, running)

    def iterate(step_at, keep):
        orthonormalize(keep)
        sent = gather_x_begin()
        block = v_row.at[pl.ds(home, 2)]
        for e in (0, 1):
            there = v_col.at[pl.ds(4 * x + 2 * zl, 2)]
            sent.append(remote(block, there, ag1_s.at[1 + e], ag1_r.at[1 + zl], holders[e]))
        for copy in sent[::-1]:
            copy.start()
        for e in (0, 1):
            part = v_col.at[pl.ds(4 * y + 2 * e, 2)]
            remote(part, part, ag1_s.at[1], ag1_r.at[1 + e], owners[e]).wait_recv()
            for i in (2, 1, 3):
                copy = remote(part, part, agy_s.at[i, e], agy_r.at[y, e], y_dev[i])
                copy.start()
                sent.append(copy)
        forward = gather_x_forward()
        for copy in forward:
            copy.start()
        sent += forward

        @pl.when(step_at == 0)
        def _():
            load.wait()

        for i in (1, 3, 2):
            for e in (0, 1):
                part = v_col.at[pl.ds(4 * y_at[i] + 2 * e, 2)]
                remote(part, part, agy_s.at[i, e], agy_r.at[y_at[i], e], y_dev[i]).wait_recv()

        half = 64 // UNROLL
        zero = jnp.zeros((64, 256), F32)
        running = multiply_up(0, half, zero)
        sent += gather_x_finish()
        multiply_up(half, 2 * half, running)

        def pick_up(b, _):
            upper[b] = slots[last_r[b]] * has_r[b]
            return 0

        lax.fori_loop(0, 32, pick_up, 0)
        for i in (1, 2, 3, 0):
            copy = remote(
                upper.at[pl.ds(other + 4 * x_at[i], 4)], half_in.at[pl.ds(4 * x_at[i], 4)],
                rsc_s.at[i], rsc_r.at[x_at[i]], core,
            )
            copy.start()
            sent.append(copy)
        gather_core_wait()
        running = multiply_down(0, half, zero)
        for i in (2, 1, 3, 0):
            q = x_at[i]
            theirs = half_in.at[pl.ds(4 * q, 4)]
            remote(theirs, theirs, rsc_s.at[i], rsc_r.at[q], core).wait_recv()

            def add_half(b, _):
                total = upper[mine + 4 * q + b] + half_in[4 * q + b]
                if i:
                    x_send[4 * i + b] = total.astype(BF16)
                else:
                    upper[mine + 4 * q + b] = total
                return 0

            lax.fori_loop(0, 4, add_half, 0)
            if i:
                copy = remote(
                    x_send.at[pl.ds(4 * i, 4)], x_in.at[pl.ds(4 * (4 - i), 4)],
                    rsx_s.at[i], rsx_r.at[4 - i], x_dev[i],
                )
                copy.start()
                sent.append(copy)
        multiply_down(half, 2 * half, running)

        def pick_down(b, _):
            total = slots[last_c[b]] * has_c[b]
            lower[b] = total
            low_send[b] = total.astype(BF16)
            return 0

        lax.fori_loop(0, 16, pick_down, 0)
        for i in (2, 1, 3):
            copy = remote(
                low_send.at[pl.ds(4 * y_at[i], 4)], y_in.at[pl.ds(4 * (4 - i), 4)],
                rsy_s.at[i], rsy_r.at[4 - i], y_dev[i],
            )
            copy.start()
            sent.append(copy)
        for i in (1, 3, 2):
            part = x_in.at[pl.ds(4 * i, 4)]
            remote(part, part, rsx_s.at[i], rsx_r.at[i], x_dev[i]).wait_recv()

        def add_x(b, _):
            at = mine + 4 * x + b
            upper[at] = (
                upper[at]
                + x_in[4 + b].astype(F32)
                + x_in[8 + b].astype(F32)
                + x_in[12 + b].astype(F32)
            )
            return 0

        lax.fori_loop(0, 4, add_x, 0)
        copy = remote(
            upper.at[pl.ds(mine + 4 * x + 2 * (1 - zl), 2)], row_in, rsf_s.at[0], rsf_r.at[0], pair
        )
        copy.start()
        sent.append(copy)
        for i in (1, 3, 2):
            part = y_in.at[pl.ds(4 * i, 4)]
            remote(part, part, rsy_s.at[i], rsy_r.at[i], y_dev[i]).wait_recv()

        def add_y(b, _):
            col_sum[b] = (
                lower[4 * y + b]
                + y_in[4 + b].astype(F32)
                + y_in[8 + b].astype(F32)
                + y_in[12 + b].astype(F32)
            )
            return 0

        lax.fori_loop(0, 4, add_y, 0)
        for e in (0, 1):
            copy = remote(
                col_sum.at[pl.ds(2 * e, 2)], col_in.at[zh], rsf_s.at[1 + e], rsf_r.at[1 + zh], owners[e]
            )
            copy.start()
            sent.append(copy)
        carried = dot_high(fact[:, 0:64], prev[...])
        remote(row_in, row_in, rsf_s.at[0], rsf_r.at[0], pair).wait_recv()
        for e in (0, 1):
            part = col_in.at[e]
            remote(part, part, rsf_s.at[1 + e], rsf_r.at[1 + e], holders[e]).wait_recv()
        for b in (0, 1):
            applied = upper[home + b] + row_in[b] + col_in[0, b] + col_in[1, b]
            wq[pl.ds(0, 64), 256 * b : 256 * b + 256] = applied - carried[:, 256 * b : 256 * b + 256]
        for copy in sent:
            copy.wait_send()

    def keep_in_loop(step_at):
        def keep(which, value):
            @pl.when(step_at > 0)
            def _():
                if which == 0:
                    alphas[step_at - 1] = value.T
                else:
                    betas[step_at - 1] = value

        return keep

    def body(step_at, _):
        iterate(step_at, keep_in_loop(step_at))
        return 0

    lax.fori_loop(0, ITERS, body, 0)

    def keep_last(which, value):
        if which == 0:
            alphas[ITERS - 1] = value.T
        else:
            betas[ITERS - 1] = value

    orthonormalize(keep_last)
    sent = gather_x_begin()
    for copy in sent:
        copy.start()
    forward = gather_x_forward()
    for copy in forward:
        copy.start()
    sent += forward + gather_x_finish()
    gather_core_wait()
    final[...] = v_row[...]
    for copy in sent:
        copy.wait_send()


def order_by(keys, others, blocks):
    count = keys.shape[0]
    at = jnp.arange(count, dtype=jnp.int32)
    unique = keys * count + at
    rank = jnp.sum((unique[None, :] < unique[:, None]).astype(jnp.int32), axis=1)
    here = (rank[None, :] == at[:, None]).astype(jnp.int32)
    perm = jnp.sum(here * at[None, :], axis=1)
    other = jnp.sum(here * others[None, :], axis=1)
    dest = jnp.sum(here * keys[None, :], axis=1)
    before = jnp.concatenate([jnp.full((1,), -1, jnp.int32), dest[:-1]])
    keep = (dest == before).astype(F32)
    block = jnp.arange(blocks, dtype=jnp.int32)
    upto = jnp.sum((keys[None, :] <= block[:, None]).astype(jnp.int32), axis=1)
    has = jnp.any(keys[None, :] == block[:, None], axis=1).astype(F32)
    return perm, other, keep, jnp.maximum(upto - 1, 0), has


def shards(start_block, tile_values, tile_rows, tile_cols):
    tiles = tile_values[0, 0]
    rows, cols = tile_rows[0, 0], tile_cols[0, 0]
    by_row = order_by(rows, cols, 32)
    by_col = order_by(cols, rows, 16)
    smem = pl.BlockSpec(memory_space=pltpu.SMEM)
    vmem = pl.BlockSpec(memory_space=pltpu.VMEM)
    hbm = pl.BlockSpec(memory_space=pl.ANY)
    dma = pltpu.SemaphoreType.DMA
    alphas, betas, final = pl.pallas_call(
        kernel,
        out_shape=[
            jax.ShapeDtypeStruct((ITERS, 64, 64), F32),
            jax.ShapeDtypeStruct((ITERS, 64, 64), F32),
            jax.ShapeDtypeStruct((32, 64, 256), BF16),
        ],
        in_specs=[smem] * 10 + [hbm, hbm],
        out_specs=[vmem] * 3,
        scratch_shapes=[
            pltpu.VMEM((128, 256, 256), BF16),
            pltpu.VMEM((128, 64, 256), F32),
            pltpu.VMEM((32, 64, 256), BF16),
            pltpu.VMEM((16, 64, 256), BF16),
            pltpu.VMEM((32, 64, 256), F32),
            pltpu.VMEM((16, 64, 256), F32),
            pltpu.VMEM((16, 64, 256), BF16),
            pltpu.VMEM((16, 64, 256), F32),
            pltpu.VMEM((16, 64, 256), BF16),
            pltpu.VMEM((16, 64, 256), BF16),
            pltpu.VMEM((16, 64, 256), BF16),
            pltpu.VMEM((2, 64, 256), F32),
            pltpu.VMEM((2, 2, 64, 256), F32),
            pltpu.VMEM((4, 64, 256), F32),
            pltpu.VMEM((128, 512), F32),
            pltpu.VMEM((64, 512), F32),
            pltpu.VMEM((64, 128), F32),
            pltpu.VMEM((16, 4, 128), F32),
            pltpu.VMEM((16, 4, 128), F32),
            pltpu.VMEM((8, 4, 128), F32),
            pltpu.VMEM((16, 4, 128), F32),
            dma, dma,
            dma((3,)), dma((3,)), dma((4, 2)), dma((4, 2)), dma((4, 2)), dma((4, 2)),
            dma((4,)), dma((4,)),
            dma((4,)), dma((4,)), dma((4,)), dma((4,)), dma((4,)), dma((4,)), dma((3,)), dma((3,)),
            dma((16,)), dma((16,)), dma((8,)), dma((8,)), dma((16,)), dma((16,)),
        ],
        compiler_params=pltpu.CompilerParams(
            collective_id=0, has_side_effects=True, vmem_limit_bytes=56 * 1024 * 1024
        ),
    )(*by_row, *by_col, start_block, tiles)
    total_rows = start_block.shape[1] * lax.axis_size("row")
    basis = final.transpose(1, 0, 2).reshape(start_block.shape).astype(F32)
    return alphas, betas, basis * math.sqrt(total_rows)


def solution(mesh):
    in_specs = (
        P(None, "row"),
        P("row", "col", None, None, None),
        P("row", "col", None),
        P("row", "col", None),
    )
    out_specs = (P(), P(), P(None, "row"))
    return jax.shard_map(shards, mesh=mesh, in_specs=in_specs, out_specs=out_specs, check_vma=False)
```

```python
import math

import jax
import jax.numpy as jnp
from jax import lax
from jax.experimental import pallas as pl
from jax.experimental.pallas import tpu as pltpu
from jax.sharding import PartitionSpec as P

ITERS = 3
HIGH = lax.Precision.HIGHEST
MESH = pl.DeviceIdType.MESH
F32 = jnp.float32
BF16 = jnp.bfloat16
NT = (((1,), (1,)), ((), ()))
NN = (((1,), (0,)), ((), ()))
UNROLL = 16


def dot_high(a, b, dims=NN):
    return lax.dot_general(a, b, dims, precision=HIGH, preferred_element_type=F32)


def factor_rows(rows):
    lane = lax.broadcasted_iota(jnp.int32, (8, 128), 1)
    sub = lax.broadcasted_iota(jnp.int32, (8, 128), 0)
    for j in range(64):
        at, inner = divmod(j, 8)
        pivot_row = rows[at][inner : inner + 1, :]
        inverse = 1.0 / pivot_row[:, j : j + 1]
        for i in range(at, 8):
            scale = jnp.broadcast_to(rows[i][:, j : j + 1] * inverse, (8, 128))
            if i == at:
                scale = jnp.where(sub > inner, scale, 0.0)
            rows[i] = rows[i] - scale * pivot_row
    done = []
    for i in range(8):
        diagonal = jnp.sum(jnp.where(lane == sub + 8 * i, rows[i], 0.0), axis=1, keepdims=True)
        scaled = rows[i] * lax.rsqrt(diagonal)
        done.append(jnp.where((lane < sub + 8 * i) & (lane < 64), 0.0, scaled))
    return done


def order_by(keys, others):
    lane = lax.broadcasted_iota(jnp.int32, (128, 128), 1)
    sub = lax.broadcasted_iota(jnp.int32, (128, 128), 0)
    key_l = jnp.broadcast_to(keys, (128, 128))
    key_s = key_l.T
    other_s = jnp.broadcast_to(others, (128, 128)).T
    smaller = (key_l * 128 + lane) < (key_s * 128 + sub)
    rank = jnp.sum(smaller.astype(jnp.int32), axis=1, keepdims=True)

    def pick(hit, values):
        return jnp.sum(jnp.where(hit, values, 0), axis=0, keepdims=True)

    here = rank == lane
    perm = pick(here, sub)
    other = pick(here, other_s)
    dest = pick(here, key_s)
    before = pick(rank == lane - 1, key_s)
    upto = pick(key_s <= lane, jnp.ones_like(lane))
    count = pick(key_s == lane, jnp.ones_like(lane))
    return (
        perm, other, jnp.maximum(upto - 1, 0),
        (dest == before).astype(F32), (count > 0).astype(F32),
    )


def kernel(
    tile_rows, tile_cols, start, tiles_hbm,
    alphas, betas, final,
    tiles, slots, v_r0, v_r1, v_r2, v_r3, v_c0, v_c1, v_c2, upper, lower, low_send,
    half_in, x_send, x_in, y_in, row_in, col_in, col_sum,
    wq, q_new, applied_old, offset, carried, fact, cross, q_row,
    g_send, g_one, g_two, g_two_alone, g_three,
    order_i, order_f, where_i, where_f,
    load_sem, start_sem, order_sem,
    ag1_s, ag1_r, agx_s, agx_r, agy_s, agy_r, agc_s, agc_r,
    rsc_s, rsc_r, rsx_s, rsx_r, rsy_s, rsy_r, rsf_s, rsf_r,
    g1_s, g1_r, g2_s, g2_r, g2l_s, g2l_r, g3_s, g3_r,
):
    r = lax.axis_index("row")
    c = lax.axis_index("col")
    zh, y = r // 4, r % 4
    x, zl, k = c // 4, (c // 2) % 2, c % 2
    core = (r, c + 1 - 2 * k)
    pair = (r, c + 2 - 4 * zl)
    x_at = [(x + i) % 4 for i in range(4)]
    y_at = [(y + i) % 4 for i in range(4)]
    x_dev = [(r, i * 4 + zl * 2 + k) for i in x_at]
    y_dev = [(zh * 4 + i, c) for i in y_at]
    holders = [(e * 4 + x, (zh * 2 + y // 2) * 4 + (y % 2) * 2 + (1 - k)) for e in (0, 1)]
    owners = [(2 * x + zl, y * 4 + e * 2 + (1 - k)) for e in (0, 1)]
    mine = (1 - k) * 16
    other = k * 16
    home = mine + 4 * x + 2 * zl
    top, bottom = pl.ds(0, 64), pl.ds(64, 64)
    v_row, v_col = (v_r0, v_r1, v_r2, v_r3), (v_c0, v_c1, v_c2)

    first = pltpu.make_async_copy(
        start.at[:, pl.ds(pl.multiple_of(home * 256, 512), 512)], wq.at[top, :], start_sem
    )
    first.start()
    load = pltpu.make_async_copy(tiles_hbm, tiles, load_sem)
    load.start()

    barrier = pltpu.get_barrier_semaphore()

    def greet_row(i, _):
        pl.semaphore_signal(barrier, inc=1, device_id=(r, (c + i) % 16), device_id_type=MESH)
        return 0

    def greet_col(i, _):
        pl.semaphore_signal(barrier, inc=1, device_id=((r + i) % 8, c), device_id_type=MESH)
        return 0

    lax.fori_loop(1, 16, greet_row, 0)
    lax.fori_loop(1, 8, greet_col, 0)
    for device in holders + owners:
        pl.semaphore_signal(barrier, inc=1, device_id=device, device_id_type=MESH)
    wq[bottom, :] = jnp.zeros((64, 512), F32)
    applied_old[...] = jnp.zeros_like(applied_old)
    first.wait()
    pl.semaphore_wait(barrier, 26)

    def remote(src, dst, s, d, device):
        return pltpu.make_async_remote_copy(
            src_ref=src, dst_ref=dst, send_sem=s, recv_sem=d, device_id=device, device_id_type=MESH
        )

    def each(count, do):
        def step(i, _):
            do(i)
            return 0

        lax.fori_loop(1, count, step, 0)

    def one(i):
        p = (c + i) % 16
        return remote(g_send.at[p], g_one.at[c], g1_s.at[i], g1_r.at[c], (r, p))

    def one_in(i):
        p = (c + i) % 16
        return remote(g_send.at[p], g_one.at[p], g1_s.at[i], g1_r.at[p], (r, p))

    def two(i, last):
        p = (r + i) % 8
        buffer, s, d = (g_two_alone, g2l_s, g2l_r) if last else (g_two, g2_s, g2_r)
        return remote(buffer.at[r], buffer.at[r], s.at[i], d.at[r], (p, c))

    def two_in(i, last):
        p = (r + i) % 8
        buffer, s, d = (g_two_alone, g2l_s, g2l_r) if last else (g_two, g2_s, g2_r)
        return remote(buffer.at[p], buffer.at[p], s.at[i], d.at[p], (p, c))

    def three(i):
        p = (c + i) % 16
        return remote(g_three.at[c], g_three.at[c], g3_s.at[i], g3_r.at[c], (r, p))

    def three_in(i):
        p = (c + i) % 16
        return remote(g_three.at[p], g_three.at[p], g3_s.at[i], g3_r.at[p], (r, p))

    def gram_begin():
        gram = dot_high(wq[top, :], wq[...], NT)
        for i in range(16):
            g_send[i] = gram[4 * i : 4 * i + 4, :]
        each(16, lambda i: one(i).start())
        g_one[c] = g_send[c]

    def gram_second(last=False):
        each(16, lambda i: one_in(i).wait_recv())
        (g_two_alone if last else g_two)[r] = jnp.sum(g_one[...], axis=0)
        each(8, lambda i: two(i, last).start())

    def gram_third(last=False):
        each(8, lambda i: two_in(i, last).wait_recv())
        g_three[c] = jnp.sum((g_two_alone if last else g_two)[...], axis=0)
        each(16, lambda i: three(i).start())

    def gram_end(at, last=False):
        each(16, lambda i: three_in(i).wait_recv())
        for i in range(16):
            fact[at, pl.ds(4 * i, 4), :] = g_three[i]
        turned = fact[at, :, 64:128]
        cross[at] = turned
        fact[at, :, 0:64] = fact[at, :, 0:64] - dot_high(turned, turned, NT)
        eye_r = lax.broadcasted_iota(jnp.int32, (64, 64), 0)
        eye_c = lax.broadcasted_iota(jnp.int32, (64, 64), 1)
        fact[at, :, 64:128] = (eye_r == eye_c).astype(F32)
        done = factor_rows([fact[at, 8 * i : 8 * i + 8, :] for i in range(8)])
        for i in range(8):
            fact[at, 8 * i : 8 * i + 8, :] = done[i]
        each(16, lambda i: one(i).wait_send())
        each(8, lambda i: two(i, last).wait_send())
        each(16, lambda i: three(i).wait_send())

    def place(at):
        rounded = wq[top, :].astype(BF16)
        v_row[at][home] = rounded[:, 0:256]
        v_row[at][home + 1] = rounded[:, 256:512]

    def gather_x_begin(at):
        block = v_row[at].at[pl.ds(home, 2)]
        sent = [remote(block, block, ag1_s.at[0], ag1_r.at[0], pair)]
        for i in (1, 2, 3):
            sent.append(remote(block, block, agx_s.at[i, 0], agx_r.at[x, zl], x_dev[i]))
        return sent

    def gather_x_forward(at):
        theirs = mine + 4 * x + 2 * (1 - zl)
        block = v_row[at].at[pl.ds(theirs, 2)]
        remote(block, block, ag1_s.at[0], ag1_r.at[0], pair).wait_recv()
        sent = []
        for i in (1, 2, 3):
            sent.append(remote(block, block, agx_s.at[i, 1], agx_r.at[x, 1 - zl], x_dev[i]))
        whole = v_row[at].at[pl.ds(mine + 4 * x, 4)]
        sent.append(remote(whole, whole, agc_s.at[0], agc_r.at[x], core))
        for copy in sent:
            copy.start()
        return sent

    def gather_x_finish(at):
        sent = []
        for i in (1, 3, 2):
            for e in (0, 1):
                block = v_row[at].at[pl.ds(mine + 4 * x_at[i] + 2 * e, 2)]
                remote(block, block, agx_s.at[i, 0], agx_r.at[x_at[i], e], x_dev[i]).wait_recv()
            whole = v_row[at].at[pl.ds(mine + 4 * x_at[i], 4)]
            copy = remote(whole, whole, agc_s.at[i], agc_r.at[x_at[i]], core)
            copy.start()
            sent.append(copy)
        return sent

    def gather_core_wait(at):
        for i in range(4):
            whole = v_row[at].at[pl.ds(other + 4 * x_at[i], 4)]
            remote(whole, whole, agc_s.at[i], agc_r.at[x_at[i]], core).wait_recv()

    def multiply_up(at, low, high, running):
        def step(j, acc):
            for i in range(UNROLL):
                p = j * UNROLL + i
                part = lax.dot_general(
                    v_col[at][where_i[1, p]], tiles[where_i[0, p]], NT, preferred_element_type=F32
                )
                acc = acc * where_f[0, p] + part
                slots[p] = acc
            return acc

        return lax.fori_loop(low, high, step, running)

    def multiply_down(at, low, high, running):
        def step(j, acc):
            for i in range(UNROLL):
                p = j * UNROLL + i
                part = lax.dot_general(
                    v_row[at][where_i[4, p]], tiles[where_i[3, p]], NN, preferred_element_type=F32
                )
                acc = acc * where_f[2, p] + part
                slots[p] = acc
            return acc

        return lax.fori_loop(low, high, step, running)

    gram_begin()
    by_row = order_by(tile_rows[...], tile_cols[...])
    by_col = order_by(tile_cols[...], tile_rows[...])
    order_i[...] = jnp.zeros_like(order_i)
    order_f[...] = jnp.zeros_like(order_f)
    for i in range(3):
        order_i[i : i + 1, :] = by_row[i]
        order_i[3 + i : 4 + i, :] = by_col[i]
    for i in range(2):
        order_f[i : i + 1, :] = by_row[3 + i]
        order_f[2 + i : 3 + i, :] = by_col[3 + i]
    orders = [
        pltpu.make_async_copy(order_i, where_i, order_sem.at[0]),
        pltpu.make_async_copy(order_f, where_f, order_sem.at[1]),
    ]
    for copy in orders:
        copy.start()
    gram_second(True)
    gram_third(True)
    gram_end(0, True)
    wq[top, :] = dot_high(fact[0, :, 64:128], wq[top, :])
    for copy in orders:
        copy.wait()

    def iterate(at):
        place(at)
        sent = gather_x_begin(at)
        block = v_row[at].at[pl.ds(home, 2)]
        for e in (0, 1):
            there = v_col[at].at[pl.ds(4 * x + 2 * zl, 2)]
            sent.append(remote(block, there, ag1_s.at[1 + e], ag1_r.at[1 + zl], holders[e]))
        for copy in sent[::-1]:
            copy.start()
        gram_begin()
        for e in (0, 1):
            part = v_col[at].at[pl.ds(4 * y + 2 * e, 2)]
            remote(part, part, ag1_s.at[1], ag1_r.at[1 + e], owners[e]).wait_recv()
            for i in (2, 1, 3):
                copy = remote(part, part, agy_s.at[i, e], agy_r.at[y, e], y_dev[i])
                copy.start()
                sent.append(copy)
        sent += gather_x_forward(at)

        if at == 0:
            load.wait()

        for i in (1, 3, 2):
            for e in (0, 1):
                part = v_col[at].at[pl.ds(4 * y_at[i] + 2 * e, 2)]
                remote(part, part, agy_s.at[i, e], agy_r.at[y_at[i], e], y_dev[i]).wait_recv()
        gram_second()

        half = 64 // UNROLL
        zero = jnp.zeros((64, 256), F32)
        running = multiply_up(at, 0, half, zero)
        sent += gather_x_finish(at)
        gram_third()
        multiply_up(at, half, 2 * half, running)
        gather_core_wait(at)

        def pick_up(b, _):
            upper[b] = slots[where_i[2, b]] * where_f[1, b]
            return 0

        lax.fori_loop(0, 32, pick_up, 0)
        for i in (1, 2, 3, 0):
            copy = remote(
                upper.at[pl.ds(other + 4 * x_at[i], 4)], half_in.at[pl.ds(4 * x_at[i], 4)],
                rsc_s.at[i], rsc_r.at[x_at[i]], core,
            )
            copy.start()
            sent.append(copy)
        running = multiply_down(at, 0, half, zero)
        for i in (2, 1, 3, 0):
            q = x_at[i]
            theirs = half_in.at[pl.ds(4 * q, 4)]
            remote(theirs, theirs, rsc_s.at[i], rsc_r.at[q], core).wait_recv()

            def add_half(b, _):
                total = upper[mine + 4 * q + b] + half_in[4 * q + b]
                if i:
                    x_send[4 * i + b] = total.astype(BF16)
                else:
                    upper[mine + 4 * q + b] = total
                return 0

            lax.fori_loop(0, 4, add_half, 0)
            if i:
                copy = remote(
                    x_send.at[pl.ds(4 * i, 4)], x_in.at[pl.ds(4 * (4 - i), 4)],
                    rsx_s.at[i], rsx_r.at[4 - i], x_dev[i],
                )
                copy.start()
                sent.append(copy)
        multiply_down(at, half, 2 * half, running)

        def pick_down(b, _):
            total = slots[where_i[5, b]] * where_f[3, b]
            lower[b] = total
            low_send[b] = total.astype(BF16)
            return 0

        lax.fori_loop(0, 16, pick_down, 0)
        for i in (2, 1, 3):
            copy = remote(
                low_send.at[pl.ds(4 * y_at[i], 4)], y_in.at[pl.ds(4 * (4 - i), 4)],
                rsy_s.at[i], rsy_r.at[4 - i], y_dev[i],
            )
            copy.start()
            sent.append(copy)
        for i in (1, 3, 2):
            part = x_in.at[pl.ds(4 * i, 4)]
            remote(part, part, rsx_s.at[i], rsx_r.at[i], x_dev[i]).wait_recv()

        def add_x(b, _):
            spot = mine + 4 * x + b
            upper[spot] = (
                upper[spot]
                + x_in[4 + b].astype(F32)
                + x_in[8 + b].astype(F32)
                + x_in[12 + b].astype(F32)
            )
            return 0

        lax.fori_loop(0, 4, add_x, 0)
        copy = remote(
            upper.at[pl.ds(mine + 4 * x + 2 * (1 - zl), 2)], row_in, rsf_s.at[0], rsf_r.at[0], pair
        )
        copy.start()
        sent.append(copy)
        gram_end(at)
        for i in (1, 3, 2):
            part = y_in.at[pl.ds(4 * i, 4)]
            remote(part, part, rsy_s.at[i], rsy_r.at[i], y_dev[i]).wait_recv()

        def add_y(b, _):
            col_sum[b] = (
                lower[4 * y + b]
                + y_in[4 + b].astype(F32)
                + y_in[8 + b].astype(F32)
                + y_in[12 + b].astype(F32)
            )
            return 0

        lax.fori_loop(0, 4, add_y, 0)
        for e in (0, 1):
            copy = remote(
                col_sum.at[pl.ds(2 * e, 2)], col_in.at[zh], rsf_s.at[1 + e], rsf_r.at[1 + zh], owners[e]
            )
            copy.start()
            sent.append(copy)

        turned = cross[at]
        inverse = fact[at, :, 64:128]
        old = wq[bottom, :]
        q_new[...] = dot_high(inverse, wq[top, :] - dot_high(turned, old))
        offset[...] = dot_high(inverse, dot_high(turned, applied_old[...]))
        carried[...] = dot_high(fact[at, :, 0:64], old)

        if at > 0:
            alphas[at - 1] = turned.T
            betas[at - 1] = fact[at, :, 0:64]

        wq[bottom, :] = q_new[...]
        remote(row_in, row_in, rsf_s.at[0], rsf_r.at[0], pair).wait_recv()
        for e in (0, 1):
            part = col_in.at[e]
            remote(part, part, rsf_s.at[1 + e], rsf_r.at[1 + e], holders[e]).wait_recv()
        for b in (0, 1):
            spot = pl.ds(256 * b, 256)
            product = upper[home + b] + row_in[b] + col_in[0, b] + col_in[1, b]
            applied = dot_high(inverse, product) - offset[:, spot]
            applied_old[:, spot] = applied
            wq[top, spot] = applied - carried[:, spot]
        for copy in sent:
            copy.wait_send()

    for at in range(ITERS):
        iterate(at)

    place(ITERS)
    sent = gather_x_begin(ITERS)
    for copy in sent:
        copy.start()
    gram_begin()
    sent += gather_x_forward(ITERS)
    gram_second(True)
    sent += gather_x_finish(ITERS)
    gram_third(True)
    mixed = fact[2, :, 64:128]
    parts = [mixed.astype(BF16)]
    for j in (1, 0):
        mixed = -dot_high(dot_high(mixed, cross[j + 1]), fact[j, :, 64:128])
        parts.append(mixed.astype(BF16))
    gather_core_wait(ITERS)

    def old_rows(b, _):
        total = lax.dot_general(parts[0], v_row[2][b], NN, preferred_element_type=F32)
        for j in (1, 0):
            total += lax.dot_general(parts[2 - j], v_row[j][b], NN, preferred_element_type=F32)
        q_row[b] = total.astype(BF16)
        return 0

    lax.fori_loop(0, 32, old_rows, 0)
    gram_end(ITERS, True)
    turned = cross[ITERS]
    alphas[ITERS - 1] = turned.T
    betas[ITERS - 1] = fact[ITERS, :, 0:64]
    inverse = fact[ITERS, :, 64:128]
    high = inverse.astype(BF16)
    low = (inverse - high.astype(F32)).astype(BF16)
    back = dot_high(inverse, turned).astype(BF16)
    for b in range(32):
        block = v_row[ITERS][b]
        total = lax.dot_general(high, block, NN, preferred_element_type=F32)
        total += lax.dot_general(low, block, NN, preferred_element_type=F32)
        total -= lax.dot_general(back, q_row[b], NN, preferred_element_type=F32)
        final[:, 256 * b : 256 * b + 256] = total
    for copy in sent:
        copy.wait_send()


def shards(start_block, tile_values, tile_rows, tile_cols):
    vmem = pl.BlockSpec(memory_space=pltpu.VMEM)
    hbm = pl.BlockSpec(memory_space=pl.ANY)
    dma = pltpu.SemaphoreType.DMA
    alphas, betas, final = pl.pallas_call(
        kernel,
        out_shape=[
            jax.ShapeDtypeStruct((ITERS, 64, 64), F32),
            jax.ShapeDtypeStruct((ITERS, 64, 64), F32),
            jax.ShapeDtypeStruct((64, 8192), F32),
        ],
        in_specs=[vmem, vmem, hbm, hbm],
        out_specs=[vmem] * 3,
        scratch_shapes=[
            pltpu.VMEM((128, 256, 256), BF16),
            pltpu.VMEM((128, 64, 256), F32),
            *[pltpu.VMEM((32, 64, 256), BF16)] * 4,
            *[pltpu.VMEM((16, 64, 256), BF16)] * 3,
            pltpu.VMEM((32, 64, 256), F32),
            pltpu.VMEM((16, 64, 256), F32),
            pltpu.VMEM((16, 64, 256), BF16),
            pltpu.VMEM((16, 64, 256), F32),
            pltpu.VMEM((16, 64, 256), BF16),
            pltpu.VMEM((16, 64, 256), BF16),
            pltpu.VMEM((16, 64, 256), BF16),
            pltpu.VMEM((2, 64, 256), F32),
            pltpu.VMEM((2, 2, 64, 256), F32),
            pltpu.VMEM((4, 64, 256), F32),
            pltpu.VMEM((128, 512), F32),
            pltpu.VMEM((64, 512), F32),
            pltpu.VMEM((64, 512), F32),
            pltpu.VMEM((64, 512), F32),
            pltpu.VMEM((64, 512), F32),
            pltpu.VMEM((4, 64, 128), F32),
            pltpu.VMEM((4, 64, 64), F32),
            pltpu.VMEM((32, 64, 256), BF16),
            pltpu.VMEM((16, 4, 128), F32),
            pltpu.VMEM((16, 4, 128), F32),
            pltpu.VMEM((8, 4, 128), F32),
            pltpu.VMEM((8, 4, 128), F32),
            pltpu.VMEM((16, 4, 128), F32),
            pltpu.VMEM((8, 128), jnp.int32),
            pltpu.VMEM((8, 128), F32),
            pltpu.SMEM((8, 128), jnp.int32),
            pltpu.SMEM((8, 128), F32),
            dma, dma, dma((2,)),
            dma((3,)), dma((3,)), dma((4, 2)), dma((4, 2)), dma((4, 2)), dma((4, 2)),
            dma((4,)), dma((4,)),
            dma((4,)), dma((4,)), dma((4,)), dma((4,)), dma((4,)), dma((4,)), dma((3,)), dma((3,)),
            dma((16,)), dma((16,)), dma((8,)), dma((8,)), dma((8,)), dma((8,)), dma((16,)), dma((16,)),
        ],
        compiler_params=pltpu.CompilerParams(
            collective_id=0, has_side_effects=True, vmem_limit_bytes=56 * 1024 * 1024
        ),
    )(tile_rows[0], tile_cols[0], start_block, tile_values[0, 0])
    total_rows = start_block.shape[1] * lax.axis_size("row")
    return alphas, betas, final * math.sqrt(total_rows)


def solution(mesh):
    in_specs = (
        P(None, "row"),
        P("row", "col", None, None, None),
        P("row", "col", None),
        P("row", "col", None),
    )
    out_specs = (P(), P(), P(None, "row"))
    return jax.shard_map(shards, mesh=mesh, in_specs=in_specs, out_specs=out_specs, check_vma=False)
```

```python
import math

import jax
import jax.numpy as jnp
from jax import lax
from jax.experimental import pallas as pl
from jax.experimental.pallas import tpu as pltpu
from jax.sharding import PartitionSpec as P

ITERS = 3
HIGH = lax.Precision.HIGHEST
MESH = pl.DeviceIdType.MESH
F32 = jnp.float32
BF16 = jnp.bfloat16
NT = (((1,), (1,)), ((), ()))
NN = (((1,), (0,)), ((), ()))
UNROLL = 16
OTHERS = ((0, 2), (0, 1), (0, 3), (1, 0), (1, 2), (1, 1), (1, 3))


def dot_high(a, b, dims=NN):
    return lax.dot_general(a, b, dims, precision=HIGH, preferred_element_type=F32)


def factor_rows(rows):
    lane = lax.broadcasted_iota(jnp.int32, (8, 128), 1)
    sub = lax.broadcasted_iota(jnp.int32, (8, 128), 0)
    for j in range(64):
        at, inner = divmod(j, 8)
        pivot_row = rows[at][inner : inner + 1, :]
        inverse = 1.0 / pivot_row[:, j : j + 1]
        for i in range(at, 8):
            scale = jnp.broadcast_to(rows[i][:, j : j + 1] * inverse, (8, 128))
            if i == at:
                scale = jnp.where(sub > inner, scale, 0.0)
            rows[i] = rows[i] - scale * pivot_row
    done = []
    for i in range(8):
        diagonal = jnp.sum(jnp.where(lane == sub + 8 * i, rows[i], 0.0), axis=1, keepdims=True)
        scaled = rows[i] * lax.rsqrt(diagonal)
        done.append(jnp.where((lane < sub + 8 * i) & (lane < 64), 0.0, scaled))
    return done


def order_by(keys, others):
    lane = lax.broadcasted_iota(jnp.int32, (128, 128), 1)
    sub = lax.broadcasted_iota(jnp.int32, (128, 128), 0)
    key_l = jnp.broadcast_to(keys, (128, 128))
    key_s = key_l.T
    other_s = jnp.broadcast_to(others, (128, 128)).T
    smaller = (key_l * 128 + lane) < (key_s * 128 + sub)
    rank = jnp.sum(smaller.astype(jnp.int32), axis=1, keepdims=True)

    def pick(hit, values):
        return jnp.sum(jnp.where(hit, values, 0), axis=0, keepdims=True)

    here = rank == lane
    perm = pick(here, sub)
    other = pick(here, other_s)
    dest = pick(here, key_s)
    before = pick(rank == lane - 1, key_s)
    upto = pick(key_s <= lane, jnp.ones_like(lane))
    count = pick(key_s == lane, jnp.ones_like(lane))
    return (
        perm, other, jnp.maximum(upto - 1, 0),
        (dest == before).astype(F32), (count > 0).astype(F32),
    )


def kernel(
    tile_rows, tile_cols, start, tiles_hbm,
    alphas, betas, final,
    tiles, slots, v_r0, v_r1, v_r2, v_r3, v_c0, v_c1, v_c2, upper, lower, low_send,
    half_in, x_send, x_in, y_in, col_in, col_sum,
    wq, q_new, applied_old, offset, carried, fact, cross, q_row,
    start_row, g_first, g_send, g_one, g_two, g_two_alone, g_three,
    order_i, order_f, where_i, where_f,
    load_sem, start_sem, order_sem,
    agp_s, agp_r, agx_s, agx_r, agy_s, agy_r, agc_s, agc_r,
    rsc_s, rsc_r, rsx_s, rsx_r, rsy_s, rsy_r, rsp_s, rsp_r,
    g0_s, g0_r, g1_s, g1_r, g2_s, g2_r, g2l_s, g2l_r, g3_s, g3_r,
):
    r = lax.axis_index("row")
    c = lax.axis_index("col")
    zh, y = r // 4, r % 4
    x, zl, k = c // 4, (c // 2) % 2, c % 2
    core = (r, c + 1 - 2 * k)
    x_at = [(x + i) % 4 for i in range(4)]
    owner = (2 * x + zl, ((x + y + 2 * k) % 4) * 4 + zh * 2 + (1 - k))
    holder_x = zh * 2 + y // 2
    holder = (
        zl * 4 + (x - holder_x - 2 * (1 - k) + 8) % 4,
        holder_x * 4 + (y % 2) * 2 + (1 - k),
    )

    def x_device(a, i):
        return (r, x_at[i] * 4 + ((zl + a) % 2) * 2 + k)

    def y_device(a, i):
        return (((zh + a) % 2) * 4 + (y + i) % 4, c)

    def x_spot(a, i):
        return 4 * x_at[i] + 2 * ((zl + a) % 2)

    def y_spot(a, i):
        return 4 * ((x + y + i + 2 * k) % 4) + 2 * ((zh + a) % 2)

    def slot(a, i):
        return a * 4 + i

    def slot_there(a, i):
        return a * 4 + (4 - i) % 4

    mine = (1 - k) * 16
    other = k * 16
    home = mine + 4 * x + 2 * zl
    top, bottom = pl.ds(0, 64), pl.ds(64, 64)
    v_row, v_col = (v_r0, v_r1, v_r2, v_r3), (v_c0, v_c1, v_c2)

    first = pltpu.make_async_copy(start, start_row, start_sem)
    first.start()
    load = pltpu.make_async_copy(tiles_hbm, tiles, load_sem)
    load.start()

    barrier = pltpu.get_barrier_semaphore()

    def greet_row(i, _):
        pl.semaphore_signal(barrier, inc=1, device_id=(r, (c + i) % 16), device_id_type=MESH)
        return 0

    def greet_col(i, _):
        pl.semaphore_signal(barrier, inc=1, device_id=((r + i) % 8, c), device_id_type=MESH)
        return 0

    lax.fori_loop(1, 16, greet_row, 0)
    lax.fori_loop(1, 8, greet_col, 0)
    for device in (owner, holder):
        pl.semaphore_signal(barrier, inc=1, device_id=device, device_id_type=MESH)
    wq[bottom, :] = jnp.zeros((64, 512), F32)
    applied_old[...] = jnp.zeros_like(applied_old)

    def remote(src, dst, s, d, device):
        return pltpu.make_async_remote_copy(
            src_ref=src, dst_ref=dst, send_sem=s, recv_sem=d, device_id=device, device_id_type=MESH
        )

    def each(count, do):
        def step(i, _):
            do(i)
            return 0

        lax.fori_loop(1, count, step, 0)

    def one(i):
        p = (c + i) % 16
        return remote(g_send.at[p], g_one.at[c], g1_s.at[i], g1_r.at[c], (r, p))

    def one_in(i):
        p = (c + i) % 16
        return remote(g_send.at[p], g_one.at[p], g1_s.at[i], g1_r.at[p], (r, p))

    def two(i, last):
        p = (r + i) % 8
        buffer, s, d = (g_two_alone, g2l_s, g2l_r) if last else (g_two, g2_s, g2_r)
        return remote(buffer.at[r], buffer.at[r], s.at[i], d.at[r], (p, c))

    def two_in(i, last):
        p = (r + i) % 8
        buffer, s, d = (g_two_alone, g2l_s, g2l_r) if last else (g_two, g2_s, g2_r)
        return remote(buffer.at[p], buffer.at[p], s.at[i], d.at[p], (p, c))

    def three(i):
        p = (c + i) % 16
        return remote(g_three.at[c], g_three.at[c], g3_s.at[i], g3_r.at[c], (r, p))

    def three_in(i):
        p = (c + i) % 16
        return remote(g_three.at[p], g_three.at[p], g3_s.at[i], g3_r.at[p], (r, p))

    def gram_begin():
        gram = dot_high(wq[top, :], wq[...], NT)
        for i in range(16):
            g_send[i] = gram[4 * i : 4 * i + 4, :]
        each(16, lambda i: one(i).start())
        g_one[c] = g_send[c]

    def gram_second(last=False):
        each(16, lambda i: one_in(i).wait_recv())
        (g_two_alone if last else g_two)[r] = jnp.sum(g_one[...], axis=0)
        each(8, lambda i: two(i, last).start())

    def gram_third(last=False):
        each(8, lambda i: two_in(i, last).wait_recv())
        g_three[c] = jnp.sum((g_two_alone if last else g_two)[...], axis=0)
        each(16, lambda i: three(i).start())

    def gram_end(at, last=False):
        each(16, lambda i: three_in(i).wait_recv())
        for i in range(16):
            fact[at, pl.ds(4 * i, 4), :] = g_three[i]
        turned = fact[at, :, 64:128]
        cross[at] = turned
        fact[at, :, 0:64] = fact[at, :, 0:64] - dot_high(turned, turned, NT)
        factorize(at)
        each(16, lambda i: one(i).wait_send())
        each(8, lambda i: two(i, last).wait_send())
        each(16, lambda i: three(i).wait_send())

    def factorize(at):
        eye_r = lax.broadcasted_iota(jnp.int32, (64, 64), 0)
        eye_c = lax.broadcasted_iota(jnp.int32, (64, 64), 1)
        fact[at, :, 64:128] = (eye_r == eye_c).astype(F32)
        done = factor_rows([fact[at, 8 * i : 8 * i + 8, :] for i in range(8)])
        for i in range(8):
            fact[at, 8 * i : 8 * i + 8, :] = done[i]

    def place(at):
        rounded = wq[top, :].astype(BF16)
        v_row[at][home] = rounded[:, 0:256]
        v_row[at][home + 1] = rounded[:, 256:512]

    def gather_rows_begin(at):
        block = v_row[at].at[pl.ds(home, 2)]
        return [
            remote(block, block, agx_s.at[slot(a, i)], agx_r.at[slot_there(a, i)], x_device(a, i))
            for a, i in OTHERS
        ]

    def gather_rows_finish(at):
        sent = []
        for i in (0, 1, 3, 2):
            for a in (0, 1):
                if (a, i) != (0, 0):
                    block = v_row[at].at[pl.ds(mine + x_spot(a, i), 2)]
                    remote(
                        block, block, agx_s.at[slot(a, i)], agx_r.at[slot(a, i)], x_device(a, i)
                    ).wait_recv()
            whole = v_row[at].at[pl.ds(mine + 4 * x_at[i], 4)]
            copy = remote(whole, whole, agc_s.at[i], agc_r.at[i], core)
            copy.start()
            sent.append(copy)
        return sent

    def gather_core_wait(at):
        for i in range(4):
            whole = v_row[at].at[pl.ds(other + 4 * x_at[i], 4)]
            remote(whole, whole, agc_s.at[i], agc_r.at[i], core).wait_recv()

    def multiply_up(at, low, high, running):
        def step(j, acc):
            for i in range(UNROLL):
                p = j * UNROLL + i
                part = lax.dot_general(
                    v_col[at][where_i[1, p]], tiles[where_i[0, p]], NT, preferred_element_type=F32
                )
                acc = acc * where_f[0, p] + part
                slots[p] = acc
            return acc

        return lax.fori_loop(low, high, step, running)

    def multiply_down(at, low, high, running):
        def step(j, acc):
            for i in range(UNROLL):
                p = j * UNROLL + i
                part = lax.dot_general(
                    v_row[at][where_i[4, p]], tiles[where_i[3, p]], NN, preferred_element_type=F32
                )
                acc = acc * where_f[2, p] + part
                slots[p] = acc
            return acc

        return lax.fori_loop(low, high, step, running)

    first.wait()

    def start_gram(i, acc):
        block = start_row[:, pl.ds(pl.multiple_of(i * 512, 512), 512)]
        high = block.astype(BF16)
        rest = block - high.astype(F32)
        middle = rest.astype(BF16)
        low = (rest - middle.astype(F32)).astype(BF16)
        terms = jnp.concatenate([high, middle, low], axis=0)
        return acc + lax.dot_general(terms, terms, NT, preferred_element_type=F32)

    gram = lax.fori_loop(0, 16, start_gram, jnp.zeros((192, 192), F32))
    gram = gram[0:64, :] + gram[64:128, :] + gram[128:192, :]
    gram = gram[:, 0:64] + gram[:, 64:128] + gram[:, 128:192]
    g_first[r, :, 0:64] = gram[0:32, :]
    g_first[r, :, 64:128] = gram[32:64, :]
    pl.semaphore_wait(barrier, 24)

    def zero_out(i):
        p = (r + i) % 8
        return remote(g_first.at[r], g_first.at[r], g0_s.at[i], g0_r.at[r], (p, c))

    def zero_in(i):
        p = (r + i) % 8
        return remote(g_first.at[p], g_first.at[p], g0_s.at[i], g0_r.at[p], (p, c))

    each(8, lambda i: zero_out(i).start())
    by_row = order_by(tile_rows[...], tile_cols[...])
    by_col = order_by(tile_cols[...], tile_rows[...])
    order_i[...] = jnp.zeros_like(order_i)
    order_f[...] = jnp.zeros_like(order_f)
    for i in range(3):
        order_i[i : i + 1, :] = by_row[i]
        order_i[3 + i : 4 + i, :] = by_col[i]
    for i in range(2):
        order_f[i : i + 1, :] = by_row[3 + i]
        order_f[2 + i : 3 + i, :] = by_col[3 + i]
    orders = [
        pltpu.make_async_copy(order_i, where_i, order_sem.at[0]),
        pltpu.make_async_copy(order_f, where_f, order_sem.at[1]),
    ]
    for copy in orders:
        copy.start()
    each(8, lambda i: zero_in(i).wait_recv())
    total = jnp.sum(g_first[...], axis=0)
    fact[0, 0:32, 0:64] = total[:, 0:64]
    fact[0, 32:64, 0:64] = total[:, 64:128]
    factorize(0)
    begin = start_row[:, pl.ds(pl.multiple_of(home * 256, 512), 512)]
    wq[top, :] = dot_high(fact[0, :, 64:128], begin)
    for copy in orders:
        copy.wait()
    each(8, lambda i: zero_out(i).wait_send())

    def iterate(at):
        bank = at % 2
        place(at)
        block = v_row[at].at[pl.ds(home, 2)]
        there = v_col[at].at[pl.ds(4 * x + 2 * zl, 2)]
        sent = [remote(block, there, agp_s, agp_r, holder)]
        sent += gather_rows_begin(at)
        for copy in sent:
            copy.start()
        gram_begin()
        part = v_col[at].at[pl.ds(y_spot(0, 0), 2)]
        remote(part, part, agp_s, agp_r, owner).wait_recv()
        for a, i in OTHERS:
            copy = remote(part, part, agy_s.at[slot(a, i)], agy_r.at[slot_there(a, i)], y_device(a, i))
            copy.start()
            sent.append(copy)
        sent += gather_rows_finish(at)
        if at == 0:
            load.wait()
        gather_core_wait(at)

        zero = jnp.zeros((64, 256), F32)
        multiply_down(at, 0, 128 // UNROLL, zero)

        def pick_down(b, _):
            total = slots[where_i[5, b]] * where_f[3, b]
            lower[b] = total
            low_send[b] = total.astype(BF16)
            return 0

        lax.fori_loop(0, 16, pick_down, 0)
        for a, i in OTHERS:
            copy = remote(
                low_send.at[pl.ds(y_spot(a, i), 2)], y_in.at[bank, pl.ds(2 * slot_there(a, i), 2)],
                rsy_s.at[slot(a, i)], rsy_r.at[bank, slot_there(a, i)], y_device(a, i),
            )
            copy.start()
            sent.append(copy)
        for a, i in OTHERS:
            part = v_col[at].at[pl.ds(y_spot(a, i), 2)]
            remote(
                part, part, agy_s.at[slot(a, i)], agy_r.at[slot(a, i)], y_device(a, i)
            ).wait_recv()
        gram_second()

        half = 64 // UNROLL
        running = multiply_up(at, 0, half, zero)
        gram_third()
        multiply_up(at, half, 2 * half, running)

        def pick_up(b, _):
            upper[b] = slots[where_i[2, b]] * where_f[1, b]
            return 0

        lax.fori_loop(0, 32, pick_up, 0)
        for i in (2, 1, 3, 0):
            copy = remote(
                upper.at[pl.ds(other + 4 * x_at[i], 4)], half_in.at[pl.ds(4 * x_at[i], 4)],
                rsc_s.at[i], rsc_r.at[i], core,
            )
            copy.start()
            sent.append(copy)
        for i in (2, 1, 3, 0):
            q = x_at[i]
            theirs = half_in.at[pl.ds(4 * q, 4)]
            remote(theirs, theirs, rsc_s.at[i], rsc_r.at[i], core).wait_recv()

            def add_half(b, _):
                total = upper[mine + 4 * q + b] + half_in[4 * q + b]
                x_send[4 * q + b] = total.astype(BF16)
                if i == 0:
                    upper[mine + 4 * q + b] = total
                return 0

            lax.fori_loop(0, 4, add_half, 0)
            for a in (1, 0):
                if (a, i) != (0, 0):
                    copy = remote(
                        x_send.at[pl.ds(x_spot(a, i), 2)], x_in.at[pl.ds(2 * slot_there(a, i), 2)],
                        rsx_s.at[slot(a, i)], rsx_r.at[slot_there(a, i)], x_device(a, i),
                    )
                    copy.start()
                    sent.append(copy)
        for a, i in OTHERS:
            part = y_in.at[bank, pl.ds(2 * slot(a, i), 2)]
            remote(
                part, part, rsy_s.at[slot(a, i)], rsy_r.at[bank, slot(a, i)], y_device(a, i)
            ).wait_recv()
        for b in (0, 1):
            total = lower[y_spot(0, 0) + b]
            for a, i in OTHERS:
                total = total + y_in[bank, 2 * slot(a, i) + b].astype(F32)
            col_sum[b] = total
        copy = remote(col_sum, col_in, rsp_s, rsp_r, owner)
        copy.start()
        sent.append(copy)
        gram_end(at)

        turned = cross[at]
        inverse = fact[at, :, 64:128]
        old = wq[bottom, :]
        q_new[...] = dot_high(inverse, wq[top, :] - dot_high(turned, old))
        offset[...] = dot_high(inverse, dot_high(turned, applied_old[...]))
        carried[...] = dot_high(fact[at, :, 0:64], old)
        if at > 0:
            alphas[at - 1] = turned.T
            betas[at - 1] = fact[at, :, 0:64]
        wq[bottom, :] = q_new[...]
        for a, i in OTHERS:
            part = x_in.at[pl.ds(2 * slot(a, i), 2)]
            remote(
                part, part, rsx_s.at[slot(a, i)], rsx_r.at[slot(a, i)], x_device(a, i)
            ).wait_recv()
        for b in (0, 1):
            total = upper[home + b]
            for a, i in OTHERS:
                total = total + x_in[2 * slot(a, i) + b].astype(F32)
            upper[home + b] = total
        remote(col_sum, col_in, rsp_s, rsp_r, holder).wait_recv()
        for b in (0, 1):
            spot = pl.ds(256 * b, 256)
            product = upper[home + b] + col_in[b]
            applied = dot_high(inverse, product) - offset[:, spot]
            applied_old[:, spot] = applied
            wq[top, spot] = applied - carried[:, spot]
        for copy in sent:
            copy.wait_send()

    for at in range(ITERS):
        iterate(at)

    place(ITERS)
    sent = gather_rows_begin(ITERS)
    gram_begin()
    for copy in sent:
        copy.start()
    gram_second(True)
    sent += gather_rows_finish(ITERS)
    gram_third(True)
    mixed = fact[2, :, 64:128]
    parts = [mixed.astype(BF16)]
    for j in (1, 0):
        mixed = -dot_high(dot_high(mixed, cross[j + 1]), fact[j, :, 64:128])
        parts.append(mixed.astype(BF16))
    gather_core_wait(ITERS)

    def old_rows(b, _):
        total = lax.dot_general(parts[0], v_row[2][b], NN, preferred_element_type=F32)
        for j in (1, 0):
            total += lax.dot_general(parts[2 - j], v_row[j][b], NN, preferred_element_type=F32)
        q_row[b] = total.astype(BF16)
        return 0

    lax.fori_loop(0, 32, old_rows, 0)
    gram_end(ITERS, True)
    turned = cross[ITERS]
    alphas[ITERS - 1] = turned.T
    betas[ITERS - 1] = fact[ITERS, :, 0:64]
    inverse = fact[ITERS, :, 64:128]
    high = inverse.astype(BF16)
    low = (inverse - high.astype(F32)).astype(BF16)
    back = dot_high(inverse, turned).astype(BF16)
    for b in range(32):
        block = v_row[ITERS][b]
        total = lax.dot_general(high, block, NN, preferred_element_type=F32)
        total += lax.dot_general(low, block, NN, preferred_element_type=F32)
        total -= lax.dot_general(back, q_row[b], NN, preferred_element_type=F32)
        final[:, 256 * b : 256 * b + 256] = total
    for copy in sent:
        copy.wait_send()


def shards(start_block, tile_values, tile_rows, tile_cols):
    vmem = pl.BlockSpec(memory_space=pltpu.VMEM)
    hbm = pl.BlockSpec(memory_space=pl.ANY)
    dma = pltpu.SemaphoreType.DMA
    alphas, betas, final = pl.pallas_call(
        kernel,
        out_shape=[
            jax.ShapeDtypeStruct((ITERS, 64, 64), F32),
            jax.ShapeDtypeStruct((ITERS, 64, 64), F32),
            jax.ShapeDtypeStruct((64, 8192), F32),
        ],
        in_specs=[vmem, vmem, hbm, hbm],
        out_specs=[vmem] * 3,
        scratch_shapes=[
            pltpu.VMEM((128, 256, 256), BF16),
            pltpu.VMEM((128, 64, 256), F32),
            *[pltpu.VMEM((32, 64, 256), BF16)] * 4,
            *[pltpu.VMEM((16, 64, 256), BF16)] * 3,
            pltpu.VMEM((32, 64, 256), F32),
            pltpu.VMEM((16, 64, 256), F32),
            pltpu.VMEM((16, 64, 256), BF16),
            pltpu.VMEM((16, 64, 256), F32),
            pltpu.VMEM((16, 64, 256), BF16),
            pltpu.VMEM((16, 64, 256), BF16),
            pltpu.VMEM((2, 16, 64, 256), BF16),
            pltpu.VMEM((2, 64, 256), F32),
            pltpu.VMEM((2, 64, 256), F32),
            pltpu.VMEM((128, 512), F32),
            pltpu.VMEM((64, 512), F32),
            pltpu.VMEM((64, 512), F32),
            pltpu.VMEM((64, 512), F32),
            pltpu.VMEM((64, 512), F32),
            pltpu.VMEM((4, 64, 128), F32),
            pltpu.VMEM((4, 64, 64), F32),
            pltpu.VMEM((32, 64, 256), BF16),
            pltpu.VMEM((64, 8192), F32),
            pltpu.VMEM((8, 32, 128), F32),
            pltpu.VMEM((16, 4, 128), F32),
            pltpu.VMEM((16, 4, 128), F32),
            pltpu.VMEM((8, 4, 128), F32),
            pltpu.VMEM((8, 4, 128), F32),
            pltpu.VMEM((16, 4, 128), F32),
            pltpu.VMEM((8, 128), jnp.int32),
            pltpu.VMEM((8, 128), F32),
            pltpu.SMEM((8, 128), jnp.int32),
            pltpu.SMEM((8, 128), F32),
            dma, dma, dma((2,)),
            dma, dma, dma((8,)), dma((8,)), dma((8,)), dma((8,)), dma((4,)), dma((4,)),
            dma((4,)), dma((4,)), dma((8,)), dma((8,)), dma((8,)), dma((2, 8)), dma, dma,
            dma((8,)), dma((8,)),
            dma((16,)), dma((16,)), dma((8,)), dma((8,)), dma((8,)), dma((8,)), dma((16,)), dma((16,)),
        ],
        compiler_params=pltpu.CompilerParams(
            collective_id=0, has_side_effects=True, vmem_limit_bytes=56 * 1024 * 1024
        ),
    )(tile_rows[0], tile_cols[0], start_block, tile_values[0, 0])
    total_rows = start_block.shape[1] * lax.axis_size("row")
    return alphas, betas, final * math.sqrt(total_rows)


def solution(mesh):
    in_specs = (
        P(None, "row"),
        P("row", "col", None, None, None),
        P("row", "col", None),
        P("row", "col", None),
    )
    out_specs = (P(), P(), P(None, "row"))
    return jax.shard_map(shards, mesh=mesh, in_specs=in_specs, out_specs=out_specs, check_vma=False)
```

```python
import math

import jax
import jax.numpy as jnp
from jax import lax
from jax.experimental import pallas as pl
from jax.experimental.pallas import tpu as pltpu
from jax.sharding import PartitionSpec as P

ITERS = 3
HIGH = lax.Precision.HIGHEST
MESH = pl.DeviceIdType.MESH
F32 = jnp.float32
BF16 = jnp.bfloat16
NT = (((1,), (1,)), ((), ()))
NN = (((1,), (0,)), ((), ()))
UNROLL = 32
OTHERS = ((0, 2), (0, 1), (0, 3), (1, 0), (1, 2), (1, 1), (1, 3))


def dot_high(a, b, dims=NN):
    return lax.dot_general(a, b, dims, precision=HIGH, preferred_element_type=F32)


def factor_rows(rows):
    lane = lax.broadcasted_iota(jnp.int32, (8, 128), 1)
    sub = lax.broadcasted_iota(jnp.int32, (8, 128), 0)
    for j in range(64):
        at, inner = divmod(j, 8)
        pivot_row = rows[at][inner : inner + 1, :]
        inverse = 1.0 / pivot_row[:, j : j + 1]
        for i in range(at, 8):
            scale = jnp.broadcast_to(rows[i][:, j : j + 1] * inverse, (8, 128))
            if i == at:
                scale = jnp.where(sub > inner, scale, 0.0)
            rows[i] = rows[i] - scale * pivot_row
    done = []
    for i in range(8):
        diagonal = jnp.sum(jnp.where(lane == sub + 8 * i, rows[i], 0.0), axis=1, keepdims=True)
        scaled = rows[i] * lax.rsqrt(diagonal)
        done.append(jnp.where((lane < sub + 8 * i) & (lane < 64), 0.0, scaled))
    return done


def order_by(keys, others):
    lane = lax.broadcasted_iota(jnp.int32, (128, 128), 1)
    sub = lax.broadcasted_iota(jnp.int32, (128, 128), 0)
    key_l = jnp.broadcast_to(keys, (128, 128))
    key_s = key_l.T
    other_s = jnp.broadcast_to(others, (128, 128)).T
    smaller = (key_l * 128 + lane) < (key_s * 128 + sub)
    rank = jnp.sum(smaller.astype(jnp.int32), axis=1, keepdims=True)

    def pick(hit, values):
        return jnp.sum(jnp.where(hit, values, 0), axis=0, keepdims=True)

    here = rank == lane
    perm = pick(here, sub)
    other = pick(here, other_s)
    dest = pick(here, key_s)
    before = pick(rank == lane - 1, key_s)
    upto = pick(key_s <= lane, jnp.ones_like(lane))
    count = pick(key_s == lane, jnp.ones_like(lane))
    return (
        perm, other, jnp.maximum(upto - 1, 0),
        (dest == before).astype(F32), (count > 0).astype(F32),
    )


def kernel(
    tile_rows, tile_cols, start, tiles_hbm,
    alphas, betas, factors, last_rows, old_rows,
    tiles, slots, v_r0, v_r1, v_r2, v_r3, v_c0, v_c1, v_c2, upper, lower, low_send,
    half_in, x_send, x_in, y_in, col_in, col_sum,
    wq, q_new, applied_old, offset, carried, fact, cross, q_row,
    start_row, start_col, g_first, g_send, g_one, g_two, g_three,
    order_i, order_f, where_i, where_f,
    load_sem, start_sem, order_sem, out_sem,
    sp_s, sp_r, sy_s, sy_r,
    agp_s, agp_r, agx_s, agx_r, agy_s, agy_r, agc_s, agc_r,
    rsc_s, rsc_r, rsx_s, rsx_r, rsy_s, rsy_r, rsp_s, rsp_r,
    g0_s, g0_r, g1_s, g1_r, g2_s, g2_r, g3_s, g3_r,
):
    r = lax.axis_index("row")
    c = lax.axis_index("col")
    zh, y = r // 4, r % 4
    x, zl, k = c // 4, (c // 2) % 2, c % 2
    core = (r, c + 1 - 2 * k)
    x_at = [(x + i) % 4 for i in range(4)]
    owner = (2 * x + zl, ((x + y + 2 * k) % 4) * 4 + zh * 2 + (1 - k))
    holder_x = zh * 2 + y // 2
    holder = (
        zl * 4 + (x - holder_x - 2 * (1 - k) + 8) % 4,
        holder_x * 4 + (y % 2) * 2 + (1 - k),
    )

    def x_device(a, i):
        return (r, x_at[i] * 4 + ((zl + a) % 2) * 2 + k)

    def y_device(a, i):
        return (((zh + a) % 2) * 4 + (y + i) % 4, c)

    def x_spot(a, i):
        return 4 * x_at[i] + 2 * ((zl + a) % 2)

    def y_spot(a, i):
        return 4 * ((x + y + i + 2 * k) % 4) + 2 * ((zh + a) % 2)

    def slot(a, i):
        return a * 4 + i

    def slot_there(a, i):
        return a * 4 + (4 - i) % 4

    mine = (1 - k) * 16
    other = k * 16
    home = mine + 4 * x + 2 * zl
    top, bottom = pl.ds(0, 64), pl.ds(64, 64)
    v_row, v_col = (v_r0, v_r1, v_r2, v_r3), (v_c0, v_c1, v_c2)

    first = pltpu.make_async_copy(start, start_row, start_sem)
    first.start()
    load = pltpu.make_async_copy(tiles_hbm, tiles, load_sem)

    barrier = pltpu.get_barrier_semaphore()

    def greet_row(i, _):
        pl.semaphore_signal(barrier, inc=1, device_id=(r, (c + i) % 16), device_id_type=MESH)
        return 0

    def greet_col(i, _):
        pl.semaphore_signal(barrier, inc=1, device_id=((r + i) % 8, c), device_id_type=MESH)
        return 0

    lax.fori_loop(1, 16, greet_row, 0)
    lax.fori_loop(1, 8, greet_col, 0)
    for device in (owner, holder):
        pl.semaphore_signal(barrier, inc=1, device_id=device, device_id_type=MESH)

    def remote(src, dst, s, d, device):
        return pltpu.make_async_remote_copy(
            src_ref=src, dst_ref=dst, send_sem=s, recv_sem=d, device_id=device, device_id_type=MESH
        )

    def each(count, do):
        def step(i, _):
            do(i)
            return 0

        lax.fori_loop(1, count, step, 0)

    def one(i):
        p = (c + i) % 16
        return remote(g_send.at[p], g_one.at[c], g1_s.at[i], g1_r.at[c], (r, p))

    def one_in(i):
        p = (c + i) % 16
        return remote(g_send.at[p], g_one.at[p], g1_s.at[i], g1_r.at[p], (r, p))

    def two(i, bank):
        p = (r + i) % 8
        return remote(g_two.at[bank, r], g_two.at[bank, r], g2_s.at[i], g2_r.at[bank, r], (p, c))

    def two_in(i, bank):
        p = (r + i) % 8
        return remote(g_two.at[bank, p], g_two.at[bank, p], g2_s.at[i], g2_r.at[bank, p], (p, c))

    def three(i):
        p = (c + i) % 16
        return remote(g_three.at[c], g_three.at[c], g3_s.at[i], g3_r.at[c], (r, p))

    def three_in(i):
        p = (c + i) % 16
        return remote(g_three.at[p], g_three.at[p], g3_s.at[i], g3_r.at[p], (r, p))

    def gram_begin():
        gram = dot_high(wq[top, :], wq[...], NT)
        for i in range(16):
            g_send[i] = gram[4 * i : 4 * i + 4, :]
        each(16, lambda i: one(i).start())
        g_one[c] = g_send[c]

    def gram_second(bank):
        each(16, lambda i: one_in(i).wait_recv())
        g_two[bank, r] = jnp.sum(g_one[...], axis=0)
        each(8, lambda i: two(i, bank).start())

    def gram_third(bank):
        each(8, lambda i: two_in(i, bank).wait_recv())
        g_three[c] = jnp.sum(g_two[bank], axis=0)
        each(16, lambda i: three(i).start())

    def gram_end(at):
        each(16, lambda i: three_in(i).wait_recv())
        for i in range(16):
            fact[at, pl.ds(4 * i, 4), :] = g_three[i]
        turned = fact[at, :, 64:128]
        cross[at] = turned
        fact[at, :, 0:64] = fact[at, :, 0:64] - dot_high(turned, turned, NT)
        factorize(at)
        each(16, lambda i: one(i).wait_send())
        each(8, lambda i: two(i, at - 1).wait_send())
        each(16, lambda i: three(i).wait_send())

    def factorize(at):
        eye_r = lax.broadcasted_iota(jnp.int32, (64, 64), 0)
        eye_c = lax.broadcasted_iota(jnp.int32, (64, 64), 1)
        fact[at, :, 64:128] = (eye_r == eye_c).astype(F32)
        done = factor_rows([fact[at, 8 * i : 8 * i + 8, :] for i in range(8)])
        for i in range(8):
            fact[at, 8 * i : 8 * i + 8, :] = done[i]

    def place(at):
        rounded = wq[top, :].astype(BF16)
        v_row[at][home] = rounded[:, 0:256]
        v_row[at][home + 1] = rounded[:, 256:512]

    def gather_rows_begin(at):
        block = v_row[at].at[pl.ds(home, 2)]
        return [
            remote(block, block, agx_s.at[slot(a, i)], agx_r.at[slot_there(a, i)], x_device(a, i))
            for a, i in OTHERS
        ]

    def gather_rows_finish(at):
        sent = []
        for i in (0, 1, 3, 2):
            for a in (0, 1):
                if (a, i) != (0, 0):
                    block = v_row[at].at[pl.ds(mine + x_spot(a, i), 2)]
                    remote(
                        block, block, agx_s.at[slot(a, i)], agx_r.at[slot(a, i)], x_device(a, i)
                    ).wait_recv()
            whole = v_row[at].at[pl.ds(mine + 4 * x_at[i], 4)]
            copy = remote(whole, whole, agc_s.at[i], agc_r.at[i], core)
            copy.start()
            sent.append(copy)
        return sent

    def gather_core_wait(at):
        for i in range(4):
            whole = v_row[at].at[pl.ds(other + 4 * x_at[i], 4)]
            remote(whole, whole, agc_s.at[i], agc_r.at[i], core).wait_recv()

    def multiply_up(at, low, high, running):
        def step(j, acc):
            for i in range(UNROLL):
                p = j * UNROLL + i
                part = lax.dot_general(
                    v_col[at][where_i[1, p]], tiles[where_i[0, p]], NT, preferred_element_type=F32
                )
                acc = acc * where_f[0, p] + part
                slots[p] = acc
            return acc

        return lax.fori_loop(low, high, step, running)

    def multiply_down(at, low, high, running):
        def step(j, acc):
            for i in range(UNROLL):
                p = j * UNROLL + i
                part = lax.dot_general(
                    v_row[at][where_i[4, p]], tiles[where_i[3, p]], NN, preferred_element_type=F32
                )
                acc = acc * where_f[2, p] + part
                slots[p] = acc
            return acc

        return lax.fori_loop(low, high, step, running)

    first.wait()
    load.start()

    pl.semaphore_wait(barrier, 24)
    lanes = lambda spot: pl.ds(pl.multiple_of(spot * 256, 512), 512)
    raw_sent = [
        remote(
            start_row.at[:, lanes(home)], start_col.at[:, lanes(4 * x + 2 * zl)], sp_s, sp_r, holder
        )
    ]
    raw_sent[0].start()

    def start_gram(i, acc):
        block = start_row[:, pl.ds(pl.multiple_of(i * 512, 512), 512)]
        high = block.astype(BF16)
        rest = block - high.astype(F32)
        middle = rest.astype(BF16)
        low = (rest - middle.astype(F32)).astype(BF16)
        terms = jnp.concatenate([high, middle, low], axis=0)
        return acc + lax.dot_general(terms, terms, NT, preferred_element_type=F32)

    gram = lax.fori_loop(0, 16, start_gram, jnp.zeros((192, 192), F32))
    gram = gram[0:64, :] + gram[64:128, :] + gram[128:192, :]
    gram = gram[:, 0:64] + gram[:, 64:128] + gram[:, 128:192]
    g_first[r, :, 0:64] = gram[0:32, :]
    g_first[r, :, 64:128] = gram[32:64, :]

    def zero_out(i):
        p = (r + i) % 8
        return remote(g_first.at[r], g_first.at[r], g0_s.at[i], g0_r.at[r], (p, c))

    def zero_in(i):
        p = (r + i) % 8
        return remote(g_first.at[p], g_first.at[p], g0_s.at[i], g0_r.at[p], (p, c))

    each(8, lambda i: zero_out(i).start())
    by_row = order_by(tile_rows[...], tile_cols[...])
    by_col = order_by(tile_cols[...], tile_rows[...])
    order_i[...] = jnp.zeros_like(order_i)
    order_f[...] = jnp.zeros_like(order_f)
    for i in range(3):
        order_i[i : i + 1, :] = by_row[i]
        order_i[3 + i : 4 + i, :] = by_col[i]
    for i in range(2):
        order_f[i : i + 1, :] = by_row[3 + i]
        order_f[2 + i : 3 + i, :] = by_col[3 + i]
    orders = [
        pltpu.make_async_copy(order_i, where_i, order_sem.at[0]),
        pltpu.make_async_copy(order_f, where_f, order_sem.at[1]),
    ]
    for copy in orders:
        copy.start()
    chunk = start_col.at[:, lanes(y_spot(0, 0))]
    remote(chunk, chunk, sp_s, sp_r, owner).wait_recv()
    for a, i in OTHERS:
        copy = remote(chunk, chunk, sy_s.at[slot(a, i)], sy_r.at[slot_there(a, i)], y_device(a, i))
        copy.start()
        raw_sent.append(copy)
    each(8, lambda i: zero_in(i).wait_recv())
    total = jnp.sum(g_first[...], axis=0)
    fact[0, 0:32, 0:64] = total[:, 0:64]
    fact[0, 32:64, 0:64] = total[:, 64:128]
    factorize(0)
    inverse = fact[0, :, 64:128]
    wq[top, :] = dot_high(inverse, start_row[:, lanes(home)])
    high = inverse.astype(BF16)
    low = (inverse - high.astype(F32)).astype(BF16)
    left = jnp.concatenate([high, high, low], axis=1)

    def solve(source, target, count):
        def step(b, _):
            block = source[:, pl.ds(pl.multiple_of(b * 256, 256), 256)]
            upper_half = block.astype(BF16)
            lower_half = (block - upper_half.astype(F32)).astype(BF16)
            right = jnp.concatenate([upper_half, lower_half, upper_half], axis=0)
            target[b] = lax.dot_general(left, right, NN, preferred_element_type=F32).astype(BF16)
            return 0

        lax.fori_loop(0, count, step, 0, unroll=4)

    solve(start_row, v_row[0], 32)
    for copy in orders:
        copy.wait()
    each(8, lambda i: zero_out(i).wait_send())

    def iterate(at):
        sent = []
        if at == 0:
            load.wait()
        else:
            place(at)
            block = v_row[at].at[pl.ds(home, 2)]
            there = v_col[at].at[pl.ds(4 * x + 2 * zl, 2)]
            sent.append(remote(block, there, agp_s, agp_r.at[at], holder))
            sent += gather_rows_begin(at)
            for copy in sent:
                copy.start()
            gram_begin()
            part = v_col[at].at[pl.ds(y_spot(0, 0), 2)]
            remote(part, part, agp_s, agp_r.at[at], owner).wait_recv()
            for a, i in OTHERS:
                copy = remote(
                    part, part, agy_s.at[slot(a, i)], agy_r.at[at, slot_there(a, i)], y_device(a, i)
                )
                copy.start()
                sent.append(copy)
            gram_second(at - 1)
            sent += gather_rows_finish(at)
            gather_core_wait(at)

        zero = jnp.zeros((64, 256), F32)
        multiply_down(at, 0, 128 // UNROLL, zero)

        def pick_down(b, _):
            total = slots[where_i[5, b]] * where_f[3, b]
            lower[b] = total
            low_send[b] = total.astype(BF16)
            return 0

        lax.fori_loop(0, 16, pick_down, 0)
        for a, i in OTHERS:
            copy = remote(
                low_send.at[pl.ds(y_spot(a, i), 2)], y_in.at[at, pl.ds(2 * slot_there(a, i), 2)],
                rsy_s.at[slot(a, i)], rsy_r.at[at, slot_there(a, i)], y_device(a, i),
            )
            copy.start()
            sent.append(copy)
        if at == 0:
            for a, i in OTHERS:
                part = start_col.at[:, lanes(y_spot(a, i))]
                remote(
                    part, part, sy_s.at[slot(a, i)], sy_r.at[slot(a, i)], y_device(a, i)
                ).wait_recv()
            solve(start_col, v_col[0], 16)
        else:
            gram_third(at - 1)
            for a, i in OTHERS:
                part = v_col[at].at[pl.ds(y_spot(a, i), 2)]
                remote(
                    part, part, agy_s.at[slot(a, i)], agy_r.at[at, slot(a, i)], y_device(a, i)
                ).wait_recv()
        multiply_up(at, 0, 128 // UNROLL, zero)

        def pick_up(b, _):
            upper[b] = slots[where_i[2, b]] * where_f[1, b]
            return 0

        lax.fori_loop(0, 32, pick_up, 0)
        for i in (2, 1, 3, 0):
            copy = remote(
                upper.at[pl.ds(other + 4 * x_at[i], 4)], half_in.at[pl.ds(4 * x_at[i], 4)],
                rsc_s.at[i], rsc_r.at[i], core,
            )
            copy.start()
            sent.append(copy)
        for i in (2, 1, 3, 0):
            q = x_at[i]
            theirs = half_in.at[pl.ds(4 * q, 4)]
            remote(theirs, theirs, rsc_s.at[i], rsc_r.at[i], core).wait_recv()

            def add_half(b, _):
                total = upper[mine + 4 * q + b] + half_in[4 * q + b]
                x_send[4 * q + b] = total.astype(BF16)
                if i == 0:
                    upper[mine + 4 * q + b] = total
                return 0

            lax.fori_loop(0, 4, add_half, 0)
            for a in (1, 0):
                if (a, i) != (0, 0):
                    copy = remote(
                        x_send.at[pl.ds(x_spot(a, i), 2)], x_in.at[pl.ds(2 * slot_there(a, i), 2)],
                        rsx_s.at[slot(a, i)], rsx_r.at[slot_there(a, i)], x_device(a, i),
                    )
                    copy.start()
                    sent.append(copy)
        for a, i in OTHERS:
            part = y_in.at[at, pl.ds(2 * slot(a, i), 2)]
            remote(
                part, part, rsy_s.at[slot(a, i)], rsy_r.at[at, slot(a, i)], y_device(a, i)
            ).wait_recv()
        for b in (0, 1):
            total = lower[y_spot(0, 0) + b]
            for a, i in OTHERS:
                total = total + y_in[at, 2 * slot(a, i) + b].astype(F32)
            col_sum[b] = total
        copy = remote(col_sum, col_in, rsp_s, rsp_r, owner)
        copy.start()
        sent.append(copy)
        if at == 0:
            wq[bottom, :] = wq[top, :]
        else:
            gram_end(at)
            turned = cross[at]
            inverse = fact[at, :, 64:128]
            old = wq[bottom, :]
            q_new[...] = dot_high(inverse, wq[top, :] - dot_high(turned, old))
            offset[...] = dot_high(inverse, dot_high(turned, applied_old[...]))
            carried[...] = dot_high(fact[at, :, 0:64], old)
            alphas[at - 1] = turned.T
            betas[at - 1] = fact[at, :, 0:64]
            wq[bottom, :] = q_new[...]
        for a, i in OTHERS:
            part = x_in.at[pl.ds(2 * slot(a, i), 2)]
            remote(
                part, part, rsx_s.at[slot(a, i)], rsx_r.at[slot(a, i)], x_device(a, i)
            ).wait_recv()
        for b in (0, 1):
            total = upper[home + b]
            for a, i in OTHERS:
                total = total + x_in[2 * slot(a, i) + b].astype(F32)
            upper[home + b] = total
        remote(col_sum, col_in, rsp_s, rsp_r, holder).wait_recv()
        for b in (0, 1):
            spot = pl.ds(256 * b, 256)
            product = upper[home + b] + col_in[b]
            if at == 0:
                applied_old[:, spot] = product
                wq[top, spot] = product
            else:
                applied = dot_high(inverse, product) - offset[:, spot]
                applied_old[:, spot] = applied
                wq[top, spot] = applied - carried[:, spot]
        for copy in sent:
            copy.wait_send()

    for at in range(ITERS):
        iterate(at)
    for copy in raw_sent:
        copy.wait_send()

    place(ITERS)
    sent = gather_rows_begin(ITERS)
    gram_begin()
    for copy in sent:
        copy.start()
    gram_second(ITERS - 1)
    sent += gather_rows_finish(ITERS)
    gram_third(ITERS - 1)
    mixed = fact[2, :, 64:128]
    parts = [mixed.astype(BF16)]
    mixed = -dot_high(dot_high(mixed, cross[2]), fact[1, :, 64:128])
    parts.append(mixed.astype(BF16))
    parts.append((-dot_high(mixed, cross[1])).astype(BF16))
    gather_core_wait(ITERS)
    keep_rows = pltpu.make_async_copy(v_row[ITERS], last_rows, out_sem.at[0])
    keep_rows.start()

    def combine(b, _):
        total = lax.dot_general(parts[0], v_row[2][b], NN, preferred_element_type=F32)
        total += lax.dot_general(parts[1], v_row[1][b], NN, preferred_element_type=F32)
        total += lax.dot_general(parts[2], v_row[0][b], NN, preferred_element_type=F32)
        q_row[b] = total.astype(BF16)
        return 0

    lax.fori_loop(0, 32, combine, 0, unroll=4)
    keep_old = pltpu.make_async_copy(q_row, old_rows, out_sem.at[1])
    keep_old.start()
    gram_end(ITERS)
    turned = cross[ITERS]
    alphas[ITERS - 1] = turned.T
    betas[ITERS - 1] = fact[ITERS, :, 0:64]
    inverse = fact[ITERS, :, 64:128]
    factors[0] = inverse
    factors[1] = -dot_high(inverse, turned)
    for copy in sent:
        copy.wait_send()
    keep_rows.wait()
    keep_old.wait()


def finish(alphas_in, betas_in, factors, last_rows, old_rows, alphas, betas, final):
    alphas[...] = alphas_in[...]
    betas[...] = betas_in[...]
    inverse = factors[0]
    high = inverse.astype(BF16)
    low = (inverse - high.astype(F32)).astype(BF16)
    left = jnp.concatenate([high, low, factors[1].astype(BF16)], axis=1)
    for b in range(last_rows.shape[0]):
        right = jnp.concatenate([last_rows[b], last_rows[b], old_rows[b]], axis=0)
        total = lax.dot_general(left, right, NN, preferred_element_type=F32)
        final[:, 256 * b : 256 * b + 256] = total * math.sqrt(65536)


def shards(start_block, tile_values, tile_rows, tile_cols):
    vmem = pl.BlockSpec(memory_space=pltpu.VMEM)
    hbm = pl.BlockSpec(memory_space=pl.ANY)
    dma = pltpu.SemaphoreType.DMA
    small = jax.ShapeDtypeStruct((ITERS, 64, 64), F32)
    rows_out = jax.ShapeDtypeStruct((32, 64, 256), BF16)
    alphas, betas, factors, last_rows, old_rows = pl.pallas_call(
        kernel,
        out_shape=[small, small, jax.ShapeDtypeStruct((2, 64, 64), F32), rows_out, rows_out],
        in_specs=[vmem, vmem, hbm, hbm],
        out_specs=[vmem, vmem, vmem, hbm, hbm],
        scratch_shapes=[
            pltpu.VMEM((128, 256, 256), BF16),
            pltpu.VMEM((128, 64, 256), F32),
            *[pltpu.VMEM((32, 64, 256), BF16)] * 4,
            *[pltpu.VMEM((16, 64, 256), BF16)] * 3,
            pltpu.VMEM((32, 64, 256), F32),
            pltpu.VMEM((16, 64, 256), F32),
            pltpu.VMEM((16, 64, 256), BF16),
            pltpu.VMEM((16, 64, 256), F32),
            pltpu.VMEM((16, 64, 256), BF16),
            pltpu.VMEM((16, 64, 256), BF16),
            pltpu.VMEM((3, 16, 64, 256), BF16),
            pltpu.VMEM((2, 64, 256), F32),
            pltpu.VMEM((2, 64, 256), F32),
            pltpu.VMEM((128, 512), F32),
            pltpu.VMEM((64, 512), F32),
            pltpu.VMEM((64, 512), F32),
            pltpu.VMEM((64, 512), F32),
            pltpu.VMEM((64, 512), F32),
            pltpu.VMEM((4, 64, 128), F32),
            pltpu.VMEM((4, 64, 64), F32),
            pltpu.VMEM((32, 64, 256), BF16),
            pltpu.VMEM((64, 8192), F32),
            pltpu.VMEM((64, 4096), F32),
            pltpu.VMEM((8, 32, 128), F32),
            pltpu.VMEM((16, 4, 128), F32),
            pltpu.VMEM((16, 4, 128), F32),
            pltpu.VMEM((3, 8, 4, 128), F32),
            pltpu.VMEM((16, 4, 128), F32),
            pltpu.VMEM((8, 128), jnp.int32),
            pltpu.VMEM((8, 128), F32),
            pltpu.SMEM((8, 128), jnp.int32),
            pltpu.SMEM((8, 128), F32),
            dma, dma, dma((2,)), dma((2,)),
            dma, dma, dma((8,)), dma((8,)),
            dma, dma((3,)), dma((8,)), dma((8,)), dma((8,)), dma((3, 8)), dma((4,)), dma((4,)),
            dma((4,)), dma((4,)), dma((8,)), dma((8,)), dma((8,)), dma((3, 8)), dma, dma,
            dma((8,)), dma((8,)),
            dma((16,)), dma((16,)), dma((8,)), dma((3, 8)), dma((16,)), dma((16,)),
        ],
        compiler_params=pltpu.CompilerParams(
            collective_id=0, has_side_effects=True, vmem_limit_bytes=56 * 1024 * 1024
        ),
    )(tile_rows[0], tile_cols[0], start_block, tile_values[0, 0])
    step = 8
    whole = pl.BlockSpec((ITERS, 64, 64), lambda i: (0, 0, 0))
    rows = pl.BlockSpec((step, 64, 256), lambda i: (i, 0, 0))
    return pl.pallas_call(
        finish,
        grid=(32 // step,),
        out_shape=[small, small, jax.ShapeDtypeStruct((64, 8192), F32)],
        in_specs=[whole, whole, pl.BlockSpec((2, 64, 64), lambda i: (0, 0, 0)), rows, rows],
        out_specs=[whole, whole, pl.BlockSpec((64, step * 256), lambda i: (0, i))],
    )(alphas, betas, factors, last_rows, old_rows)


def solution(mesh):
    in_specs = (
        P(None, "row"),
        P("row", "col", None, None, None),
        P("row", "col", None),
        P("row", "col", None),
    )
    out_specs = (P(), P(), P(None, "row"))
    return jax.shard_map(shards, mesh=mesh, in_specs=in_specs, out_specs=out_specs, check_vma=False)
```

```python
import math

import jax
import jax.numpy as jnp
from jax import lax
from jax.experimental import pallas as pl
from jax.experimental.pallas import tpu as pltpu
from jax.sharding import PartitionSpec as P

ITERS = 3
HIGH = lax.Precision.HIGHEST
MESH = pl.DeviceIdType.MESH
F32 = jnp.float32
BF16 = jnp.bfloat16
NT = (((1,), (1,)), ((), ()))
NN = (((1,), (0,)), ((), ()))
UNROLL = 32
OTHERS = ((0, 1), (0, 3), (1, 0), (0, 2), (1, 1), (1, 3), (1, 2))


def dot_high(a, b, dims=NN):
    return lax.dot_general(a, b, dims, precision=HIGH, preferred_element_type=F32)


def split(value):
    high = value.astype(BF16)
    return high, (value - high.astype(F32)).astype(BF16)


def left_terms(value):
    high, low = split(value)
    return jnp.concatenate([high, high, low], axis=1)


def dot_terms(left, right):
    high, low = split(right)
    return lax.dot_general(
        left, jnp.concatenate([high, low, high], axis=0), NN, preferred_element_type=F32
    )


def factor_rows(rows):
    lane = lax.broadcasted_iota(jnp.int32, (8, 128), 1)
    sub = lax.broadcasted_iota(jnp.int32, (8, 128), 0)
    for j in range(0, 64, 2):
        at, inner = divmod(j, 8)
        first = rows[at][inner : inner + 1, :]
        second = rows[at][inner + 1 : inner + 2, :]
        left = [jnp.broadcast_to(rows[i][:, j : j + 1], (8, 128)) for i in range(at, 8)]
        right = [jnp.broadcast_to(rows[i][:, j + 1 : j + 2], (8, 128)) for i in range(at, 8)]
        a = left[0][inner : inner + 1, :]
        b = left[0][inner + 1 : inner + 2, :]
        d = right[0][inner + 1 : inner + 2, :]
        inverse = 1.0 / (a * d - b * b)
        over_first = (d * first - b * second) * inverse
        over_second = (a * second - b * first) * inverse
        ratio = b * (1.0 / a)
        for i in range(at, 8):
            change = left[i - at] * over_first + right[i - at] * over_second
            if i == at:
                change = jnp.where(sub > inner + 1, change, 0.0)
                change = jnp.where(sub == inner + 1, ratio * first, change)
            rows[i] = rows[i] - change
    done = []
    for i in range(8):
        diagonal = jnp.sum(jnp.where(lane == sub + 8 * i, rows[i], 0.0), axis=1, keepdims=True)
        scaled = rows[i] * lax.rsqrt(diagonal)
        done.append(jnp.where((lane < sub + 8 * i) & (lane < 64), 0.0, scaled))
    return done


def order_by(keys, others):
    lane = lax.broadcasted_iota(jnp.int32, (128, 128), 1)
    sub = lax.broadcasted_iota(jnp.int32, (128, 128), 0)
    key_l = jnp.broadcast_to(keys, (128, 128))
    key_s = key_l.T
    other_s = jnp.broadcast_to(others, (128, 128)).T
    smaller = (key_l * 128 + lane) < (key_s * 128 + sub)
    rank = jnp.sum(smaller.astype(jnp.int32), axis=1, keepdims=True)

    def pick(hit, values):
        return jnp.sum(jnp.where(hit, values, 0), axis=0, keepdims=True)

    here = rank == lane
    perm = pick(here, sub)
    other = pick(here, other_s)
    dest = pick(here, key_s)
    before = pick(rank == lane - 1, key_s)
    upto = pick(key_s <= lane, jnp.ones_like(lane))
    count = pick(key_s == lane, jnp.ones_like(lane))
    return (
        perm, other, jnp.maximum(upto - 1, 0),
        (dest == before).astype(F32), (count > 0).astype(F32),
    )


def kernel(
    tile_rows, tile_cols, start, tiles_hbm,
    alphas, betas, factors, last_rows, old_rows,
    tiles, slots, v_r0, v_r1, v_r2, v_r3, v_c0, v_c1, v_c2, upper, lower, low_send,
    half_in, x_send, x_in, y_in, col_in, col_sum,
    wq, q_new, applied_old, offset, carried, fact, cross, q_row,
    start_row, start_own, start_col, g_first, g_send, g_one, g_two, g_three,
    order_i, order_f, where_i, where_f,
    load_sem, start_sem, order_sem, out_sem,
    sp_s, sp_r, sy_s, sy_r,
    agp_s, agp_r, agx_s, agx_r, agy_s, agy_r, agc_s, agc_r,
    rsc_s, rsc_r, rsx_s, rsx_r, rsy_s, rsy_r, rsp_s, rsp_r,
    g0_s, g0_r, g1_s, g1_r, g2_s, g2_r, g3_s, g3_r,
):
    r = lax.axis_index("row")
    c = lax.axis_index("col")
    zh, y = r // 4, r % 4
    x, zl, k = c // 4, (c // 2) % 2, c % 2
    core = (r, c + 1 - 2 * k)
    x_at = [(x + i) % 4 for i in range(4)]
    owner = (2 * x + zl, ((x + y + 2 * k) % 4) * 4 + zh * 2 + (1 - k))
    holder_x = zh * 2 + y // 2
    holder = (
        zl * 4 + (x - holder_x - 2 * (1 - k) + 8) % 4,
        holder_x * 4 + (y % 2) * 2 + (1 - k),
    )

    def x_device(a, i):
        return (r, x_at[i] * 4 + ((zl + a) % 2) * 2 + k)

    def y_device(a, i):
        return (((zh + a) % 2) * 4 + (y + i) % 4, c)

    def x_spot(a, i):
        return 4 * x_at[i] + 2 * ((zl + a) % 2)

    def y_spot(a, i):
        return 4 * ((x + y + i + 2 * k) % 4) + 2 * ((zh + a) % 2)

    def slot(a, i):
        return a * 4 + i

    def slot_there(a, i):
        return a * 4 + (4 - i) % 4

    mine = (1 - k) * 16
    other = k * 16
    home = mine + 4 * x + 2 * zl
    top, bottom = pl.ds(0, 64), pl.ds(64, 64)
    v_row, v_col = (v_r0, v_r1, v_r2, v_r3), (v_c0, v_c1, v_c2)

    first = pltpu.make_async_copy(start, start_row, start_sem)
    first.start()
    load = pltpu.make_async_copy(tiles_hbm, tiles, load_sem)

    barrier = pltpu.get_barrier_semaphore()

    def greet_row(i, _):
        pl.semaphore_signal(barrier, inc=1, device_id=(r, (c + i) % 16), device_id_type=MESH)
        return 0

    def greet_col(i, _):
        pl.semaphore_signal(barrier, inc=1, device_id=((r + i) % 8, c), device_id_type=MESH)
        return 0

    lax.fori_loop(1, 16, greet_row, 0)
    lax.fori_loop(1, 8, greet_col, 0)
    for device in (owner, holder):
        pl.semaphore_signal(barrier, inc=1, device_id=device, device_id_type=MESH)

    def remote(src, dst, s, d, device):
        return pltpu.make_async_remote_copy(
            src_ref=src, dst_ref=dst, send_sem=s, recv_sem=d, device_id=device, device_id_type=MESH
        )

    def each(count, do):
        def step(i, _):
            do(i)
            return 0

        lax.fori_loop(1, count, step, 0)

    def one(i):
        p = (c + i) % 16
        return remote(g_send.at[p], g_one.at[c], g1_s.at[i], g1_r.at[c], (r, p))

    def one_in(i):
        p = (c + i) % 16
        return remote(g_send.at[p], g_one.at[p], g1_s.at[i], g1_r.at[p], (r, p))

    def two(i, bank):
        p = (r + i) % 8
        return remote(g_two.at[bank, r], g_two.at[bank, r], g2_s.at[i], g2_r.at[bank, r], (p, c))

    def two_in(i, bank):
        p = (r + i) % 8
        return remote(g_two.at[bank, p], g_two.at[bank, p], g2_s.at[i], g2_r.at[bank, p], (p, c))

    def three(i):
        p = (c + i) % 16
        return remote(g_three.at[c], g_three.at[c], g3_s.at[i], g3_r.at[c], (r, p))

    def three_in(i):
        p = (c + i) % 16
        return remote(g_three.at[p], g_three.at[p], g3_s.at[i], g3_r.at[p], (r, p))

    def gram_begin():
        rows = jnp.concatenate(split(wq[top, :]) + split(wq[bottom, :]), axis=0)
        terms = lax.dot_general(rows[0:128], rows, NT, preferred_element_type=F32)
        terms = terms[0:64, :] + terms[64:128, :]
        gram = terms[:, 0:128] + pltpu.roll(terms[:, 0:128], 64, 1)
        cross_part = terms[:, 128:256] + pltpu.roll(terms[:, 128:256], 64, 1)
        gram = jnp.where(lax.broadcasted_iota(jnp.int32, (64, 128), 1) < 64, gram, cross_part)
        for i in range(16):
            g_send[i] = gram[4 * i : 4 * i + 4, :]
        each(16, lambda i: one(i).start())
        g_one[c] = g_send[c]

    def gram_second(bank):
        each(16, lambda i: one_in(i).wait_recv())
        g_two[bank, r] = jnp.sum(g_one[...], axis=0)
        each(8, lambda i: two(i, bank).start())

    def gram_third(bank):
        each(8, lambda i: two_in(i, bank).wait_recv())
        g_three[c] = jnp.sum(g_two[bank], axis=0)
        each(16, lambda i: three(i).start())

    def gram_end(at):
        each(16, lambda i: three_in(i).wait_recv())
        for i in range(16):
            fact[at, pl.ds(4 * i, 4), :] = g_three[i]
        turned = fact[at, :, 64:128]
        cross[at] = turned
        fact[at, :, 0:64] = fact[at, :, 0:64] - dot_high(turned, turned, NT)
        factorize(at)
        each(16, lambda i: one(i).wait_send())
        each(8, lambda i: two(i, at - 1).wait_send())
        each(16, lambda i: three(i).wait_send())

    def factorize(at):
        eye_r = lax.broadcasted_iota(jnp.int32, (64, 64), 0)
        eye_c = lax.broadcasted_iota(jnp.int32, (64, 64), 1)
        fact[at, :, 64:128] = (eye_r == eye_c).astype(F32)
        done = factor_rows([fact[at, 8 * i : 8 * i + 8, :] for i in range(8)])
        for i in range(8):
            fact[at, 8 * i : 8 * i + 8, :] = done[i]

    def place(at):
        rounded = wq[top, :].astype(BF16)
        v_row[at][home] = rounded[:, 0:256]
        v_row[at][home + 1] = rounded[:, 256:512]

    def gather_rows_begin(at):
        block = v_row[at].at[pl.ds(home, 2)]
        return [
            remote(block, block, agx_s.at[slot(a, i)], agx_r.at[slot_there(a, i)], x_device(a, i))
            for a, i in OTHERS
        ]

    def gather_rows_finish(at):
        sent = []
        for i in (0, 1, 3, 2):
            for a in (0, 1):
                if (a, i) != (0, 0):
                    block = v_row[at].at[pl.ds(mine + x_spot(a, i), 2)]
                    remote(
                        block, block, agx_s.at[slot(a, i)], agx_r.at[slot(a, i)], x_device(a, i)
                    ).wait_recv()
            whole = v_row[at].at[pl.ds(mine + 4 * x_at[i], 4)]
            copy = remote(whole, whole, agc_s.at[i], agc_r.at[i], core)
            copy.start()
            sent.append(copy)
        return sent

    def gather_core_wait(at):
        for i in range(4):
            whole = v_row[at].at[pl.ds(other + 4 * x_at[i], 4)]
            remote(whole, whole, agc_s.at[i], agc_r.at[i], core).wait_recv()

    def multiply_up(at, low, high, running):
        def step(j, acc):
            for i in range(UNROLL):
                p = j * UNROLL + i
                part = lax.dot_general(
                    v_col[at][where_i[1, p]], tiles[where_i[0, p]], NT, preferred_element_type=F32
                )
                acc = acc * where_f[0, p] + part
                slots[p] = acc
            return acc

        return lax.fori_loop(low, high, step, running)

    def multiply_down(at, low, high, running):
        def step(j, acc):
            for i in range(UNROLL):
                p = j * UNROLL + i
                part = lax.dot_general(
                    v_row[at][where_i[4, p]], tiles[where_i[3, p]], NN, preferred_element_type=F32
                )
                acc = acc * where_f[2, p] + part
                slots[p] = acc
            return acc

        return lax.fori_loop(low, high, step, running)

    first.wait()
    load.start()

    pl.semaphore_wait(barrier, 24)
    lanes = lambda spot: pl.ds(pl.multiple_of(spot * 256, 512), 512)
    own = start_row[:, lanes(home)]
    start_own[0] = own[:, 0:256]
    start_own[1] = own[:, 256:512]
    raw_sent = [remote(start_own, start_col.at[pl.ds(4 * x + 2 * zl, 2)], sp_s, sp_r, holder)]
    raw_sent[0].start()

    def start_gram(i, acc):
        block = start_row[:, pl.ds(pl.multiple_of(i * 512, 512), 512)]
        high = block.astype(BF16)
        low = (block - high.astype(F32)).astype(BF16)
        terms = jnp.concatenate([high, low], axis=0)
        return acc + lax.dot_general(terms, terms, NT, preferred_element_type=F32)

    gram = lax.fori_loop(0, 16, start_gram, jnp.zeros((128, 128), F32), unroll=4)
    gram = gram[0:64, :] + gram[64:128, :]
    gram = gram[:, 0:64] + gram[:, 64:128]
    g_first[r, :, 0:64] = gram[0:32, :]
    g_first[r, :, 64:128] = gram[32:64, :]

    def zero_out(i):
        p = (r + i) % 8
        return remote(g_first.at[r], g_first.at[r], g0_s.at[i], g0_r.at[r], (p, c))

    def zero_in(i):
        p = (r + i) % 8
        return remote(g_first.at[p], g_first.at[p], g0_s.at[i], g0_r.at[p], (p, c))

    each(8, lambda i: zero_out(i).start())
    by_row = order_by(tile_rows[...], tile_cols[...])
    by_col = order_by(tile_cols[...], tile_rows[...])
    order_i[...] = jnp.zeros_like(order_i)
    order_f[...] = jnp.zeros_like(order_f)
    for i in range(3):
        order_i[i : i + 1, :] = by_row[i]
        order_i[3 + i : 4 + i, :] = by_col[i]
    for i in range(2):
        order_f[i : i + 1, :] = by_row[3 + i]
        order_f[2 + i : 3 + i, :] = by_col[3 + i]
    orders = [
        pltpu.make_async_copy(order_i, where_i, order_sem.at[0]),
        pltpu.make_async_copy(order_f, where_f, order_sem.at[1]),
    ]
    for copy in orders:
        copy.start()
    chunk = start_col.at[pl.ds(y_spot(0, 0), 2)]
    remote(chunk, chunk, sp_s, sp_r, owner).wait_recv()
    for a, i in OTHERS:
        copy = remote(chunk, chunk, sy_s.at[slot(a, i)], sy_r.at[slot_there(a, i)], y_device(a, i))
        copy.start()
        raw_sent.append(copy)
    each(8, lambda i: zero_in(i).wait_recv())
    total = jnp.sum(g_first[...], axis=0)
    fact[0, 0:32, 0:64] = total[:, 0:64]
    fact[0, 32:64, 0:64] = total[:, 64:128]
    factorize(0)
    inverse = fact[0, :, 64:128]
    wq[top, :] = dot_high(inverse, start_row[:, lanes(home)])
    left = left_terms(inverse)

    def solve(source, target, count):
        def step(b, _):
            target[b] = dot_terms(left, source(b)).astype(BF16)
            return 0

        lax.fori_loop(0, count, step, 0, unroll=4)

    solve(lambda b: start_row[:, pl.ds(pl.multiple_of(b * 256, 256), 256)], v_row[0], 32)
    for copy in orders:
        copy.wait()
    each(8, lambda i: zero_out(i).wait_send())

    def iterate(at, pending):
        sent = []
        reduced = []
        if at == 0:
            load.wait()
        else:
            place(at)
            block = v_row[at].at[pl.ds(home, 2)]
            there = v_col[at].at[pl.ds(4 * x + 2 * zl, 2)]
            sent.append(remote(block, there, agp_s, agp_r.at[at], holder))
            sent += gather_rows_begin(at)
            for copy in sent:
                copy.start()
            for copy in pending:
                copy.wait_send()
            gram_begin()
            part = v_col[at].at[pl.ds(y_spot(0, 0), 2)]
            remote(part, part, agp_s, agp_r.at[at], owner).wait_recv()
            for a, i in OTHERS:
                copy = remote(
                    part, part, agy_s.at[slot(a, i)], agy_r.at[at, slot_there(a, i)], y_device(a, i)
                )
                copy.start()
                sent.append(copy)
            gram_second(at - 1)
            sent += gather_rows_finish(at)
            gather_core_wait(at)

        zero = jnp.zeros((64, 256), F32)
        multiply_down(at, 0, 128 // UNROLL, zero)

        def pick_down(b, _):
            total = slots[where_i[5, b]] * where_f[3, b]
            lower[b] = total
            low_send[b] = total.astype(BF16)
            return 0

        lax.fori_loop(0, 16, pick_down, 0)
        for a, i in OTHERS:
            copy = remote(
                low_send.at[pl.ds(y_spot(a, i), 2)], y_in.at[at, pl.ds(2 * slot_there(a, i), 2)],
                rsy_s.at[slot(a, i)], rsy_r.at[at, slot_there(a, i)], y_device(a, i),
            )
            copy.start()
            reduced.append(copy)
        if at == 0:
            for a, i in OTHERS:
                part = start_col.at[pl.ds(y_spot(a, i), 2)]
                remote(
                    part, part, sy_s.at[slot(a, i)], sy_r.at[slot(a, i)], y_device(a, i)
                ).wait_recv()
            solve(lambda b: start_col[b], v_col[0], 16)
        else:
            gram_third(at - 1)
            for a, i in OTHERS:
                part = v_col[at].at[pl.ds(y_spot(a, i), 2)]
                remote(
                    part, part, agy_s.at[slot(a, i)], agy_r.at[at, slot(a, i)], y_device(a, i)
                ).wait_recv()
        multiply_up(at, 0, 128 // UNROLL, zero)

        def pick_up(b, _):
            upper[b] = slots[where_i[2, b]] * where_f[1, b]
            return 0

        lax.fori_loop(0, 32, pick_up, 0)
        for i in (2, 1, 3, 0):
            copy = remote(
                upper.at[pl.ds(other + 4 * x_at[i], 4)], half_in.at[pl.ds(4 * x_at[i], 4)],
                rsc_s.at[i], rsc_r.at[i], core,
            )
            copy.start()
            reduced.append(copy)
        for i in (2, 1, 3, 0):
            q = x_at[i]
            theirs = half_in.at[pl.ds(4 * q, 4)]
            remote(theirs, theirs, rsc_s.at[i], rsc_r.at[i], core).wait_recv()

            def add_half(b, _):
                total = upper[mine + 4 * q + b] + half_in[4 * q + b]
                x_send[4 * q + b] = total.astype(BF16)
                if i == 0:
                    upper[mine + 4 * q + b] = total
                return 0

            lax.fori_loop(0, 4, add_half, 0)
            for a in (1, 0):
                if (a, i) != (0, 0):
                    copy = remote(
                        x_send.at[pl.ds(x_spot(a, i), 2)], x_in.at[pl.ds(2 * slot_there(a, i), 2)],
                        rsx_s.at[slot(a, i)], rsx_r.at[slot_there(a, i)], x_device(a, i),
                    )
                    copy.start()
                    reduced.append(copy)
        for a, i in OTHERS:
            part = y_in.at[at, pl.ds(2 * slot(a, i), 2)]
            remote(
                part, part, rsy_s.at[slot(a, i)], rsy_r.at[at, slot(a, i)], y_device(a, i)
            ).wait_recv()
        for b in (0, 1):
            total = lower[y_spot(0, 0) + b]
            for a, i in OTHERS:
                total = total + y_in[at, 2 * slot(a, i) + b].astype(F32)
            col_sum[b] = total
        copy = remote(col_sum, col_in, rsp_s, rsp_r, owner)
        copy.start()
        reduced.append(copy)
        if at == 0:
            wq[bottom, :] = wq[top, :]
        else:
            gram_end(at)
            turned = cross[at]
            inverse = fact[at, :, 64:128]
            terms = left_terms(inverse)
            old = wq[bottom, :]
            q_new[...] = dot_high(inverse, wq[top, :] - dot_high(turned, old))
            offset[...] = dot_high(inverse, dot_high(turned, applied_old[...]))
            carried[...] = dot_high(fact[at, :, 0:64], old)
            alphas[at - 1] = turned.T
            betas[at - 1] = fact[at, :, 0:64]
            wq[bottom, :] = q_new[...]
        for a, i in OTHERS:
            part = x_in.at[pl.ds(2 * slot(a, i), 2)]
            remote(
                part, part, rsx_s.at[slot(a, i)], rsx_r.at[slot(a, i)], x_device(a, i)
            ).wait_recv()
        for b in (0, 1):
            total = upper[home + b]
            for a, i in OTHERS:
                total = total + x_in[2 * slot(a, i) + b].astype(F32)
            upper[home + b] = total
        remote(col_sum, col_in, rsp_s, rsp_r, holder).wait_recv()
        for b in (0, 1):
            spot = pl.ds(256 * b, 256)
            product = upper[home + b] + col_in[b]
            if at == 0:
                applied_old[:, spot] = product
                wq[top, spot] = product
            else:
                applied = dot_terms(terms, product) - offset[:, spot]
                applied_old[:, spot] = applied
                wq[top, spot] = applied - carried[:, spot]
        for copy in sent:
            copy.wait_send()
        return reduced

    pending = []
    for at in range(ITERS):
        pending = iterate(at, pending)
    for copy in raw_sent:
        copy.wait_send()

    place(ITERS)
    sent = gather_rows_begin(ITERS)
    gram_begin()
    for copy in sent:
        copy.start()
    for copy in pending:
        copy.wait_send()
    gram_second(ITERS - 1)
    sent += gather_rows_finish(ITERS)
    gram_third(ITERS - 1)
    mixed = fact[2, :, 64:128]
    parts = [mixed.astype(BF16)]
    mixed = -dot_high(dot_high(mixed, cross[2]), fact[1, :, 64:128])
    parts.append(mixed.astype(BF16))
    parts.append((-dot_high(mixed, cross[1])).astype(BF16))
    gather_core_wait(ITERS)
    keep_rows = pltpu.make_async_copy(v_row[ITERS], last_rows, out_sem.at[0])
    keep_rows.start()

    def combine(b, _):
        total = lax.dot_general(parts[0], v_row[2][b], NN, preferred_element_type=F32)
        total += lax.dot_general(parts[1], v_row[1][b], NN, preferred_element_type=F32)
        total += lax.dot_general(parts[2], v_row[0][b], NN, preferred_element_type=F32)
        q_row[b] = total.astype(BF16)
        return 0

    lax.fori_loop(0, 32, combine, 0, unroll=4)
    keep_old = pltpu.make_async_copy(q_row, old_rows, out_sem.at[1])
    keep_old.start()
    gram_end(ITERS)
    turned = cross[ITERS]
    alphas[ITERS - 1] = turned.T
    betas[ITERS - 1] = fact[ITERS, :, 0:64]
    inverse = fact[ITERS, :, 64:128]
    factors[0] = inverse
    factors[1] = -dot_high(inverse, turned)
    for copy in sent:
        copy.wait_send()
    keep_rows.wait()
    keep_old.wait()


def finish(alphas_in, betas_in, factors, last_rows, old_rows, alphas, betas, final):
    alphas[...] = alphas_in[...]
    betas[...] = betas_in[...]
    inverse = factors[0]
    high = inverse.astype(BF16)
    low = (inverse - high.astype(F32)).astype(BF16)
    left = jnp.concatenate([high, low, factors[1].astype(BF16)], axis=1)
    for b in range(last_rows.shape[0]):
        right = jnp.concatenate([last_rows[b], last_rows[b], old_rows[b]], axis=0)
        total = lax.dot_general(left, right, NN, preferred_element_type=F32)
        final[:, 256 * b : 256 * b + 256] = total * math.sqrt(65536)


def shards(start_block, tile_values, tile_rows, tile_cols):
    vmem = pl.BlockSpec(memory_space=pltpu.VMEM)
    hbm = pl.BlockSpec(memory_space=pl.ANY)
    dma = pltpu.SemaphoreType.DMA
    small = jax.ShapeDtypeStruct((ITERS, 64, 64), F32)
    rows_out = jax.ShapeDtypeStruct((32, 64, 256), BF16)
    alphas, betas, factors, last_rows, old_rows = pl.pallas_call(
        kernel,
        out_shape=[small, small, jax.ShapeDtypeStruct((2, 64, 64), F32), rows_out, rows_out],
        in_specs=[vmem, vmem, hbm, hbm],
        out_specs=[vmem, vmem, vmem, hbm, hbm],
        scratch_shapes=[
            pltpu.VMEM((128, 256, 256), BF16),
            pltpu.VMEM((128, 64, 256), F32),
            *[pltpu.VMEM((32, 64, 256), BF16)] * 4,
            *[pltpu.VMEM((16, 64, 256), BF16)] * 3,
            pltpu.VMEM((32, 64, 256), F32),
            pltpu.VMEM((16, 64, 256), F32),
            pltpu.VMEM((16, 64, 256), BF16),
            pltpu.VMEM((16, 64, 256), F32),
            pltpu.VMEM((16, 64, 256), BF16),
            pltpu.VMEM((16, 64, 256), BF16),
            pltpu.VMEM((3, 16, 64, 256), BF16),
            pltpu.VMEM((2, 64, 256), F32),
            pltpu.VMEM((2, 64, 256), F32),
            pltpu.VMEM((128, 512), F32),
            pltpu.VMEM((64, 512), F32),
            pltpu.VMEM((64, 512), F32),
            pltpu.VMEM((64, 512), F32),
            pltpu.VMEM((64, 512), F32),
            pltpu.VMEM((4, 64, 128), F32),
            pltpu.VMEM((4, 64, 64), F32),
            pltpu.VMEM((32, 64, 256), BF16),
            pltpu.VMEM((64, 8192), F32),
            pltpu.VMEM((2, 64, 256), F32),
            pltpu.VMEM((16, 64, 256), F32),
            pltpu.VMEM((8, 32, 128), F32),
            pltpu.VMEM((16, 4, 128), F32),
            pltpu.VMEM((16, 4, 128), F32),
            pltpu.VMEM((3, 8, 4, 128), F32),
            pltpu.VMEM((16, 4, 128), F32),
            pltpu.VMEM((8, 128), jnp.int32),
            pltpu.VMEM((8, 128), F32),
            pltpu.SMEM((8, 128), jnp.int32),
            pltpu.SMEM((8, 128), F32),
            dma, dma, dma((2,)), dma((2,)),
            dma, dma, dma((8,)), dma((8,)),
            dma, dma((3,)), dma((8,)), dma((8,)), dma((8,)), dma((3, 8)), dma((4,)), dma((4,)),
            dma((4,)), dma((4,)), dma((8,)), dma((8,)), dma((8,)), dma((3, 8)), dma, dma,
            dma((8,)), dma((8,)),
            dma((16,)), dma((16,)), dma((8,)), dma((3, 8)), dma((16,)), dma((16,)),
        ],
        compiler_params=pltpu.CompilerParams(
            collective_id=0, has_side_effects=True, vmem_limit_bytes=56 * 1024 * 1024
        ),
    )(tile_rows[0], tile_cols[0], start_block, tile_values[0, 0])
    step = 16
    whole = pl.BlockSpec((ITERS, 64, 64), lambda i: (0, 0, 0))
    rows = pl.BlockSpec((step, 64, 256), lambda i: (i, 0, 0))
    return pl.pallas_call(
        finish,
        grid=(32 // step,),
        out_shape=[small, small, jax.ShapeDtypeStruct((64, 8192), F32)],
        in_specs=[whole, whole, pl.BlockSpec((2, 64, 64), lambda i: (0, 0, 0)), rows, rows],
        out_specs=[whole, whole, pl.BlockSpec((64, step * 256), lambda i: (0, i))],
    )(alphas, betas, factors, last_rows, old_rows)


def solution(mesh):
    in_specs = (
        P(None, "row"),
        P("row", "col", None, None, None),
        P("row", "col", None),
        P("row", "col", None),
    )
    out_specs = (P(), P(), P(None, "row"))
    return jax.shard_map(shards, mesh=mesh, in_specs=in_specs, out_specs=out_specs, check_vma=False)
```

```python
import math

import jax
import jax.numpy as jnp
from jax import lax
from jax.experimental import pallas as pl
from jax.experimental.pallas import tpu as pltpu
from jax.sharding import PartitionSpec as P

ITERS = 3
HIGH = lax.Precision.HIGHEST
MESH = pl.DeviceIdType.MESH
F32 = jnp.float32
BF16 = jnp.bfloat16
NT = (((1,), (1,)), ((), ()))
NN = (((1,), (0,)), ((), ()))
UNROLL = 32
OTHERS = ((0, 1), (0, 3), (1, 0), (0, 2), (1, 1), (1, 3), (1, 2))


def dot_high(a, b, dims=NN):
    return lax.dot_general(a, b, dims, precision=HIGH, preferred_element_type=F32)


def split(value):
    high = value.astype(BF16)
    return high, (value - high.astype(F32)).astype(BF16)


def left_terms(value):
    high, low = split(value)
    return jnp.concatenate([high, high, low], axis=1)


def dot_terms(left, right):
    high, low = split(right)
    return lax.dot_general(
        left, jnp.concatenate([high, low, high], axis=0), NN, preferred_element_type=F32
    )


def factor_rows(rows):
    lane = lax.broadcasted_iota(jnp.int32, (8, 128), 1)
    sub = lax.broadcasted_iota(jnp.int32, (8, 128), 0)
    for j in range(0, 64, 2):
        at, inner = divmod(j, 8)
        first = rows[at][inner : inner + 1, :]
        second = rows[at][inner + 1 : inner + 2, :]
        left = [jnp.broadcast_to(rows[i][:, j : j + 1], (8, 128)) for i in range(at, 8)]
        right = [jnp.broadcast_to(rows[i][:, j + 1 : j + 2], (8, 128)) for i in range(at, 8)]
        a = left[0][inner : inner + 1, :]
        b = left[0][inner + 1 : inner + 2, :]
        d = right[0][inner + 1 : inner + 2, :]
        inverse = 1.0 / (a * d - b * b)
        over_first = (d * first - b * second) * inverse
        over_second = (a * second - b * first) * inverse
        ratio = b * (1.0 / a)
        for i in range(at, 8):
            change = left[i - at] * over_first + right[i - at] * over_second
            if i == at:
                change = jnp.where(sub > inner + 1, change, 0.0)
                change = jnp.where(sub == inner + 1, ratio * first, change)
            rows[i] = rows[i] - change
    done = []
    for i in range(8):
        diagonal = jnp.sum(jnp.where(lane == sub + 8 * i, rows[i], 0.0), axis=1, keepdims=True)
        scaled = rows[i] * lax.rsqrt(diagonal)
        done.append(jnp.where((lane < sub + 8 * i) & (lane < 64), 0.0, scaled))
    return done


def order_by(keys, others):
    lane = lax.broadcasted_iota(jnp.int32, (128, 128), 1)
    sub = lax.broadcasted_iota(jnp.int32, (128, 128), 0)
    key_l = jnp.broadcast_to(keys, (128, 128))
    key_s = key_l.T
    other_s = jnp.broadcast_to(others, (128, 128)).T
    smaller = (key_l * 128 + lane) < (key_s * 128 + sub)
    rank = jnp.sum(smaller.astype(jnp.int32), axis=1, keepdims=True)

    def pick(hit, values):
        return jnp.sum(jnp.where(hit, values, 0), axis=0, keepdims=True)

    here = rank == lane
    perm = pick(here, sub)
    other = pick(here, other_s)
    dest = pick(here, key_s)
    before = pick(rank == lane - 1, key_s)
    upto = pick(key_s <= lane, jnp.ones_like(lane))
    count = pick(key_s == lane, jnp.ones_like(lane))
    return (
        perm, other, jnp.maximum(upto - 1, 0),
        (dest == before).astype(F32), (count > 0).astype(F32),
    )


def kernel(
    tile_rows, tile_cols, start, tiles_hbm,
    alphas, betas, factors, last_rows, old_rows,
    tiles, slots, v_r0, v_r1, v_r2, v_r3, v_c0, v_c1, v_c2, upper, lower, low_send,
    half_in, x_send, x_in, y_in, col_in, col_sum,
    wq, q_new, applied_old, offset, carried, fact, cross, q_row,
    start_row, start_own, start_col, g_first, g_send, g_one, g_two, g_three,
    order_i, order_f, where_i, where_f,
    load_sem, start_sem, order_sem, out_sem,
    sp_s, sp_r, sy_s, sy_r,
    agp_s, agp_r, agx_s, agx_r, agy_s, agy_r, agc_s, agc_r,
    rsc_s, rsc_r, rsx_s, rsx_r, rsy_s, rsy_r, rsp_s, rsp_r,
    g0_s, g0_r, g1_s, g1_r, g2_s, g2_r, g3_s, g3_r,
):
    r = lax.axis_index("row")
    c = lax.axis_index("col")
    zh, y = r // 4, r % 4
    x, zl, k = c // 4, (c // 2) % 2, c % 2
    core = (r, c + 1 - 2 * k)
    x_at = [(x + i) % 4 for i in range(4)]
    owner = (2 * x + zl, ((x + y + 2 * k) % 4) * 4 + zh * 2 + (1 - k))
    holder_x = zh * 2 + y // 2
    holder = (
        zl * 4 + (x - holder_x - 2 * (1 - k) + 8) % 4,
        holder_x * 4 + (y % 2) * 2 + (1 - k),
    )

    def x_device(a, i):
        return (r, x_at[i] * 4 + ((zl + a) % 2) * 2 + k)

    def y_device(a, i):
        return (((zh + a) % 2) * 4 + (y + i) % 4, c)

    def x_spot(a, i):
        return 4 * x_at[i] + 2 * ((zl + a) % 2)

    def y_spot(a, i):
        return 4 * ((x + y + i + 2 * k) % 4) + 2 * ((zh + a) % 2)

    def slot(a, i):
        return a * 4 + i

    def slot_there(a, i):
        return a * 4 + (4 - i) % 4

    mine = (1 - k) * 16
    other = k * 16
    home = mine + 4 * x + 2 * zl
    top, bottom = pl.ds(0, 64), pl.ds(64, 64)
    v_row, v_col = (v_r0, v_r1, v_r2, v_r3), (v_c0, v_c1, v_c2)

    first = pltpu.make_async_copy(start, start_row, start_sem)
    first.start()
    load = pltpu.make_async_copy(tiles_hbm, tiles, load_sem)

    barrier = pltpu.get_barrier_semaphore()

    def greet_row(i, _):
        pl.semaphore_signal(barrier, inc=1, device_id=(r, (c + i) % 16), device_id_type=MESH)
        return 0

    def greet_col(i, _):
        pl.semaphore_signal(barrier, inc=1, device_id=((r + i) % 8, c), device_id_type=MESH)
        return 0

    lax.fori_loop(1, 16, greet_row, 0)
    lax.fori_loop(1, 8, greet_col, 0)
    for device in (owner, holder):
        pl.semaphore_signal(barrier, inc=1, device_id=device, device_id_type=MESH)

    def remote(src, dst, s, d, device):
        return pltpu.make_async_remote_copy(
            src_ref=src, dst_ref=dst, send_sem=s, recv_sem=d, device_id=device, device_id_type=MESH
        )

    def each(count, do):
        def step(i, _):
            do(i)
            return 0

        lax.fori_loop(1, count, step, 0)

    def one(i):
        p = (c + i) % 16
        return remote(g_send.at[p], g_one.at[c], g1_s.at[i], g1_r.at[c], (r, p))

    def one_in(i):
        p = (c + i) % 16
        return remote(g_send.at[p], g_one.at[p], g1_s.at[i], g1_r.at[p], (r, p))

    def two(i, bank):
        p = (r + i) % 8
        return remote(g_two.at[bank, r], g_two.at[bank, r], g2_s.at[i], g2_r.at[bank, r], (p, c))

    def two_in(i, bank):
        p = (r + i) % 8
        return remote(g_two.at[bank, p], g_two.at[bank, p], g2_s.at[i], g2_r.at[bank, p], (p, c))

    def three(i):
        p = (c + i) % 16
        return remote(g_three.at[c], g_three.at[c], g3_s.at[i], g3_r.at[c], (r, p))

    def three_in(i):
        p = (c + i) % 16
        return remote(g_three.at[p], g_three.at[p], g3_s.at[i], g3_r.at[p], (r, p))

    def gram_begin():
        rows = jnp.concatenate(split(wq[top, :]) + split(wq[bottom, :]), axis=0)
        terms = lax.dot_general(rows[0:128], rows, NT, preferred_element_type=F32)
        terms = terms[0:64, :] + terms[64:128, :]
        gram = terms[:, 0:128] + pltpu.roll(terms[:, 0:128], 64, 1)
        cross_part = terms[:, 128:256] + pltpu.roll(terms[:, 128:256], 64, 1)
        gram = jnp.where(lax.broadcasted_iota(jnp.int32, (64, 128), 1) < 64, gram, cross_part)
        for i in range(16):
            g_send[i] = gram[4 * i : 4 * i + 4, :]
        each(16, lambda i: one(i).start())
        g_one[c] = g_send[c]

    def gram_second(bank):
        each(16, lambda i: one_in(i).wait_recv())
        g_two[bank, r] = jnp.sum(g_one[...], axis=0)
        each(8, lambda i: two(i, bank).start())

    def gram_third(bank):
        each(8, lambda i: two_in(i, bank).wait_recv())
        g_three[c] = jnp.sum(g_two[bank], axis=0)
        each(16, lambda i: three(i).start())

    def gram_end(at):
        each(16, lambda i: three_in(i).wait_recv())
        for i in range(16):
            fact[at, pl.ds(4 * i, 4), :] = g_three[i]
        turned = fact[at, :, 64:128]
        cross[at] = turned
        fact[at, :, 0:64] = fact[at, :, 0:64] - dot_high(turned, turned, NT)
        factorize(at)
        each(16, lambda i: one(i).wait_send())
        each(8, lambda i: two(i, at - 1).wait_send())
        each(16, lambda i: three(i).wait_send())

    def factorize(at):
        eye_r = lax.broadcasted_iota(jnp.int32, (64, 64), 0)
        eye_c = lax.broadcasted_iota(jnp.int32, (64, 64), 1)
        fact[at, :, 64:128] = (eye_r == eye_c).astype(F32)
        done = factor_rows([fact[at, 8 * i : 8 * i + 8, :] for i in range(8)])
        for i in range(8):
            fact[at, 8 * i : 8 * i + 8, :] = done[i]

    def place(at):
        rounded = wq[top, :].astype(BF16)
        v_row[at][home] = rounded[:, 0:256]
        v_row[at][home + 1] = rounded[:, 256:512]

    def gather_rows_begin(at):
        block = v_row[at].at[pl.ds(home, 2)]
        return [
            remote(block, block, agx_s.at[slot(a, i)], agx_r.at[slot_there(a, i)], x_device(a, i))
            for a, i in ((1, 0), (0, 1), (0, 3), (0, 2))
        ]

    def gather_rows_forward(at):
        block = v_row[at].at[pl.ds(mine + x_spot(1, 0), 2)]
        s, d = agx_s.at[slot(1, 0)], agx_r.at[slot(1, 0)]
        remote(block, block, s, d, x_device(1, 0)).wait_recv()
        sent = [
            remote(block, block, agx_s.at[slot(1, i)], agx_r.at[slot_there(1, i)], x_device(0, i))
            for i in (1, 3, 2)
        ]
        for copy in sent:
            copy.start()
        return sent

    def gather_rows_finish(at):
        sent = []
        for i in (0, 1, 3, 2):
            for a in (0, 1):
                if i > 0:
                    block = v_row[at].at[pl.ds(mine + x_spot(a, i), 2)]
                    remote(
                        block, block, agx_s.at[slot(a, i)], agx_r.at[slot(a, i)], x_device(a, i)
                    ).wait_recv()
            whole = v_row[at].at[pl.ds(mine + 4 * x_at[i], 4)]
            copy = remote(whole, whole, agc_s.at[i], agc_r.at[i], core)
            copy.start()
            sent.append(copy)
        return sent

    def gather_core_wait(at):
        for i in range(4):
            whole = v_row[at].at[pl.ds(other + 4 * x_at[i], 4)]
            remote(whole, whole, agc_s.at[i], agc_r.at[i], core).wait_recv()

    def multiply_up(at, low, high, running):
        def step(j, acc):
            for i in range(UNROLL):
                p = j * UNROLL + i
                part = lax.dot_general(
                    v_col[at][where_i[1, p]], tiles[where_i[0, p]], NT, preferred_element_type=F32
                )
                acc = acc * where_f[0, p] + part
                slots[p] = acc
            return acc

        return lax.fori_loop(low, high, step, running)

    def multiply_down(at, low, high, running):
        def step(j, acc):
            for i in range(UNROLL):
                p = j * UNROLL + i
                part = lax.dot_general(
                    v_row[at][where_i[4, p]], tiles[where_i[3, p]], NN, preferred_element_type=F32
                )
                acc = acc * where_f[2, p] + part
                slots[p] = acc
            return acc

        return lax.fori_loop(low, high, step, running)

    first.wait()
    load.start()

    pl.semaphore_wait(barrier, 24)
    lanes = lambda spot: pl.ds(pl.multiple_of(spot * 256, 512), 512)
    own = start_row[:, lanes(home)]
    start_own[0] = own[:, 0:256]
    start_own[1] = own[:, 256:512]
    raw_sent = [remote(start_own, start_col.at[pl.ds(4 * x + 2 * zl, 2)], sp_s, sp_r, holder)]
    raw_sent[0].start()

    def start_gram(i, acc):
        block = start_row[:, pl.ds(pl.multiple_of(i * 512, 512), 512)]
        high = block.astype(BF16)
        low = (block - high.astype(F32)).astype(BF16)
        terms = jnp.concatenate([high, low], axis=0)
        return acc + lax.dot_general(terms, terms, NT, preferred_element_type=F32)

    gram = lax.fori_loop(0, 16, start_gram, jnp.zeros((128, 128), F32), unroll=4)
    gram = gram[0:64, :] + gram[64:128, :]
    gram = gram[:, 0:64] + gram[:, 64:128]
    g_first[r, :, 0:64] = gram[0:32, :]
    g_first[r, :, 64:128] = gram[32:64, :]

    def zero_out(i):
        p = (r + i) % 8
        return remote(g_first.at[r], g_first.at[r], g0_s.at[i], g0_r.at[r], (p, c))

    def zero_in(i):
        p = (r + i) % 8
        return remote(g_first.at[p], g_first.at[p], g0_s.at[i], g0_r.at[p], (p, c))

    each(8, lambda i: zero_out(i).start())
    by_row = order_by(tile_rows[...], tile_cols[...])
    by_col = order_by(tile_cols[...], tile_rows[...])
    order_i[...] = jnp.zeros_like(order_i)
    order_f[...] = jnp.zeros_like(order_f)
    for i in range(3):
        order_i[i : i + 1, :] = by_row[i]
        order_i[3 + i : 4 + i, :] = by_col[i]
    for i in range(2):
        order_f[i : i + 1, :] = by_row[3 + i]
        order_f[2 + i : 3 + i, :] = by_col[3 + i]
    orders = [
        pltpu.make_async_copy(order_i, where_i, order_sem.at[0]),
        pltpu.make_async_copy(order_f, where_f, order_sem.at[1]),
    ]
    for copy in orders:
        copy.start()
    chunk = start_col.at[pl.ds(y_spot(0, 0), 2)]
    remote(chunk, chunk, sp_s, sp_r, owner).wait_recv()
    for a, i in ((1, 0), (0, 1), (0, 3), (0, 2)):
        copy = remote(chunk, chunk, sy_s.at[slot(a, i)], sy_r.at[slot_there(a, i)], y_device(a, i))
        copy.start()
        raw_sent.append(copy)
    each(8, lambda i: zero_in(i).wait_recv())
    chunk = start_col.at[pl.ds(y_spot(1, 0), 2)]
    remote(chunk, chunk, sy_s.at[slot(1, 0)], sy_r.at[slot(1, 0)], y_device(1, 0)).wait_recv()
    for i in (1, 3, 2):
        copy = remote(chunk, chunk, sy_s.at[slot(1, i)], sy_r.at[slot_there(1, i)], y_device(0, i))
        copy.start()
        raw_sent.append(copy)
    total = jnp.sum(g_first[...], axis=0)
    fact[0, 0:32, 0:64] = total[:, 0:64]
    fact[0, 32:64, 0:64] = total[:, 64:128]
    factorize(0)
    inverse = fact[0, :, 64:128]
    wq[top, :] = dot_high(inverse, start_row[:, lanes(home)])
    left = left_terms(inverse)

    def solve(source, target, count):
        def step(b, _):
            target[b] = dot_terms(left, source(b)).astype(BF16)
            return 0

        lax.fori_loop(0, count, step, 0, unroll=4)

    solve(lambda b: start_row[:, pl.ds(pl.multiple_of(b * 256, 256), 256)], v_row[0], 32)
    for copy in orders:
        copy.wait()
    each(8, lambda i: zero_out(i).wait_send())

    def iterate(at, pending):
        sent = []
        reduced = []
        if at == 0:
            load.wait()
        else:
            place(at)
            block = v_row[at].at[pl.ds(home, 2)]
            there = v_col[at].at[pl.ds(4 * x + 2 * zl, 2)]
            sent.append(remote(block, there, agp_s, agp_r.at[at], holder))
            sent += gather_rows_begin(at)
            for copy in sent:
                copy.start()
            for copy in pending:
                copy.wait_send()
            gram_begin()
            sent += gather_rows_forward(at)
            part = v_col[at].at[pl.ds(y_spot(0, 0), 2)]
            remote(part, part, agp_s, agp_r.at[at], owner).wait_recv()
            for a, i in OTHERS:
                copy = remote(
                    part, part, agy_s.at[slot(a, i)], agy_r.at[at, slot_there(a, i)], y_device(a, i)
                )
                copy.start()
                sent.append(copy)
            gram_second(at - 1)
            sent += gather_rows_finish(at)
            gather_core_wait(at)

        zero = jnp.zeros((64, 256), F32)
        multiply_down(at, 0, 128 // UNROLL, zero)

        def pick_down(b, _):
            total = slots[where_i[5, b]] * where_f[3, b]
            lower[b] = total
            low_send[b] = total.astype(BF16)
            return 0

        lax.fori_loop(0, 16, pick_down, 0)
        for a, i in OTHERS:
            copy = remote(
                low_send.at[pl.ds(y_spot(a, i), 2)], y_in.at[at, pl.ds(2 * slot_there(a, i), 2)],
                rsy_s.at[slot(a, i)], rsy_r.at[at, slot_there(a, i)], y_device(a, i),
            )
            copy.start()
            reduced.append(copy)
        if at == 0:
            for a, i in ((0, 1), (0, 3), (0, 2), (1, 1), (1, 3), (1, 2)):
                part = start_col.at[pl.ds(y_spot(a, i), 2)]
                remote(
                    part, part, sy_s.at[slot(a, i)], sy_r.at[slot(a, i)], y_device(a, i)
                ).wait_recv()
            solve(lambda b: start_col[b], v_col[0], 16)
        else:
            gram_third(at - 1)
            for a, i in OTHERS:
                part = v_col[at].at[pl.ds(y_spot(a, i), 2)]
                remote(
                    part, part, agy_s.at[slot(a, i)], agy_r.at[at, slot(a, i)], y_device(a, i)
                ).wait_recv()
        multiply_up(at, 0, 128 // UNROLL, zero)

        def pick_up(b, _):
            upper[b] = slots[where_i[2, b]] * where_f[1, b]
            return 0

        lax.fori_loop(0, 32, pick_up, 0)
        for i in (2, 1, 3, 0):
            copy = remote(
                upper.at[pl.ds(other + 4 * x_at[i], 4)], half_in.at[pl.ds(4 * x_at[i], 4)],
                rsc_s.at[i], rsc_r.at[i], core,
            )
            copy.start()
            reduced.append(copy)
        for i in (2, 1, 3, 0):
            q = x_at[i]
            theirs = half_in.at[pl.ds(4 * q, 4)]
            remote(theirs, theirs, rsc_s.at[i], rsc_r.at[i], core).wait_recv()

            def add_half(b, _):
                total = upper[mine + 4 * q + b] + half_in[4 * q + b]
                x_send[4 * q + b] = total.astype(BF16)
                if i == 0:
                    upper[mine + 4 * q + b] = total
                return 0

            lax.fori_loop(0, 4, add_half, 0)
            for a in (1, 0):
                if (a, i) != (0, 0):
                    copy = remote(
                        x_send.at[pl.ds(x_spot(a, i), 2)], x_in.at[pl.ds(2 * slot_there(a, i), 2)],
                        rsx_s.at[slot(a, i)], rsx_r.at[slot_there(a, i)], x_device(a, i),
                    )
                    copy.start()
                    reduced.append(copy)
        for a, i in OTHERS:
            part = y_in.at[at, pl.ds(2 * slot(a, i), 2)]
            remote(
                part, part, rsy_s.at[slot(a, i)], rsy_r.at[at, slot(a, i)], y_device(a, i)
            ).wait_recv()
        for b in (0, 1):
            total = lower[y_spot(0, 0) + b]
            for a, i in OTHERS:
                total = total + y_in[at, 2 * slot(a, i) + b].astype(F32)
            col_sum[b] = total
        copy = remote(col_sum, col_in, rsp_s, rsp_r, owner)
        copy.start()
        reduced.append(copy)
        if at == 0:
            wq[bottom, :] = wq[top, :]
        else:
            gram_end(at)
            turned = cross[at]
            inverse = fact[at, :, 64:128]
            terms = left_terms(inverse)
            old = wq[bottom, :]
            q_new[...] = dot_high(inverse, wq[top, :] - dot_high(turned, old))
            offset[...] = dot_high(inverse, dot_high(turned, applied_old[...]))
            carried[...] = dot_high(fact[at, :, 0:64], old)
            alphas[at - 1] = turned.T
            betas[at - 1] = fact[at, :, 0:64]
            wq[bottom, :] = q_new[...]
        for a, i in OTHERS:
            part = x_in.at[pl.ds(2 * slot(a, i), 2)]
            remote(
                part, part, rsx_s.at[slot(a, i)], rsx_r.at[slot(a, i)], x_device(a, i)
            ).wait_recv()
        for b in (0, 1):
            total = upper[home + b]
            for a, i in OTHERS:
                total = total + x_in[2 * slot(a, i) + b].astype(F32)
            upper[home + b] = total
        remote(col_sum, col_in, rsp_s, rsp_r, holder).wait_recv()
        for b in (0, 1):
            spot = pl.ds(256 * b, 256)
            product = upper[home + b] + col_in[b]
            if at == 0:
                applied_old[:, spot] = product
                wq[top, spot] = product
            else:
                applied = dot_terms(terms, product) - offset[:, spot]
                applied_old[:, spot] = applied
                wq[top, spot] = applied - carried[:, spot]
        for copy in sent:
            copy.wait_send()
        return reduced

    pending = []
    for at in range(ITERS):
        pending = iterate(at, pending)
    for copy in raw_sent:
        copy.wait_send()

    place(ITERS)
    sent = gather_rows_begin(ITERS)
    gram_begin()
    for copy in sent:
        copy.start()
    for copy in pending:
        copy.wait_send()
    sent += gather_rows_forward(ITERS)
    gram_second(ITERS - 1)
    sent += gather_rows_finish(ITERS)
    gram_third(ITERS - 1)
    mixed = fact[2, :, 64:128]
    parts = [mixed.astype(BF16)]
    mixed = -dot_high(dot_high(mixed, cross[2]), fact[1, :, 64:128])
    parts.append(mixed.astype(BF16))
    parts.append((-dot_high(mixed, cross[1])).astype(BF16))
    gather_core_wait(ITERS)
    keep_rows = pltpu.make_async_copy(v_row[ITERS], last_rows, out_sem.at[0])
    keep_rows.start()

    def combine(b, _):
        total = lax.dot_general(parts[0], v_row[2][b], NN, preferred_element_type=F32)
        total += lax.dot_general(parts[1], v_row[1][b], NN, preferred_element_type=F32)
        total += lax.dot_general(parts[2], v_row[0][b], NN, preferred_element_type=F32)
        q_row[b] = total.astype(BF16)
        return 0

    lax.fori_loop(0, 32, combine, 0, unroll=4)
    keep_old = pltpu.make_async_copy(q_row, old_rows, out_sem.at[1])
    keep_old.start()
    gram_end(ITERS)
    turned = cross[ITERS]
    alphas[ITERS - 1] = turned.T
    betas[ITERS - 1] = fact[ITERS, :, 0:64]
    inverse = fact[ITERS, :, 64:128]
    factors[0] = inverse
    factors[1] = -dot_high(inverse, turned)
    for copy in sent:
        copy.wait_send()
    keep_rows.wait()
    keep_old.wait()


def finish(alphas_in, betas_in, factors, last_rows, old_rows, alphas, betas, final):
    alphas[...] = alphas_in[...]
    betas[...] = betas_in[...]
    inverse = factors[0]
    high = inverse.astype(BF16)
    low = (inverse - high.astype(F32)).astype(BF16)
    left = jnp.concatenate([high, low, factors[1].astype(BF16)], axis=1)
    for b in range(last_rows.shape[0]):
        right = jnp.concatenate([last_rows[b], last_rows[b], old_rows[b]], axis=0)
        total = lax.dot_general(left, right, NN, preferred_element_type=F32)
        final[:, 256 * b : 256 * b + 256] = total * math.sqrt(65536)


def shards(start_block, tile_values, tile_rows, tile_cols):
    vmem = pl.BlockSpec(memory_space=pltpu.VMEM)
    hbm = pl.BlockSpec(memory_space=pl.ANY)
    dma = pltpu.SemaphoreType.DMA
    small = jax.ShapeDtypeStruct((ITERS, 64, 64), F32)
    rows_out = jax.ShapeDtypeStruct((32, 64, 256), BF16)
    alphas, betas, factors, last_rows, old_rows = pl.pallas_call(
        kernel,
        out_shape=[small, small, jax.ShapeDtypeStruct((2, 64, 64), F32), rows_out, rows_out],
        in_specs=[vmem, vmem, hbm, hbm],
        out_specs=[vmem, vmem, vmem, hbm, hbm],
        scratch_shapes=[
            pltpu.VMEM((128, 256, 256), BF16),
            pltpu.VMEM((128, 64, 256), F32),
            *[pltpu.VMEM((32, 64, 256), BF16)] * 4,
            *[pltpu.VMEM((16, 64, 256), BF16)] * 3,
            pltpu.VMEM((32, 64, 256), F32),
            pltpu.VMEM((16, 64, 256), F32),
            pltpu.VMEM((16, 64, 256), BF16),
            pltpu.VMEM((16, 64, 256), F32),
            pltpu.VMEM((16, 64, 256), BF16),
            pltpu.VMEM((16, 64, 256), BF16),
            pltpu.VMEM((3, 16, 64, 256), BF16),
            pltpu.VMEM((2, 64, 256), F32),
            pltpu.VMEM((2, 64, 256), F32),
            pltpu.VMEM((128, 512), F32),
            pltpu.VMEM((64, 512), F32),
            pltpu.VMEM((64, 512), F32),
            pltpu.VMEM((64, 512), F32),
            pltpu.VMEM((64, 512), F32),
            pltpu.VMEM((4, 64, 128), F32),
            pltpu.VMEM((4, 64, 64), F32),
            pltpu.VMEM((32, 64, 256), BF16),
            pltpu.VMEM((64, 8192), F32),
            pltpu.VMEM((2, 64, 256), F32),
            pltpu.VMEM((16, 64, 256), F32),
            pltpu.VMEM((8, 32, 128), F32),
            pltpu.VMEM((16, 4, 128), F32),
            pltpu.VMEM((16, 4, 128), F32),
            pltpu.VMEM((3, 8, 4, 128), F32),
            pltpu.VMEM((16, 4, 128), F32),
            pltpu.VMEM((8, 128), jnp.int32),
            pltpu.VMEM((8, 128), F32),
            pltpu.SMEM((8, 128), jnp.int32),
            pltpu.SMEM((8, 128), F32),
            dma, dma, dma((2,)), dma((2,)),
            dma, dma, dma((8,)), dma((8,)),
            dma, dma((3,)), dma((8,)), dma((8,)), dma((8,)), dma((3, 8)), dma((4,)), dma((4,)),
            dma((4,)), dma((4,)), dma((8,)), dma((8,)), dma((8,)), dma((3, 8)), dma, dma,
            dma((8,)), dma((8,)),
            dma((16,)), dma((16,)), dma((8,)), dma((3, 8)), dma((16,)), dma((16,)),
        ],
        compiler_params=pltpu.CompilerParams(
            collective_id=0, has_side_effects=True, vmem_limit_bytes=56 * 1024 * 1024
        ),
    )(tile_rows[0], tile_cols[0], start_block, tile_values[0, 0])
    step = 16
    whole = pl.BlockSpec((ITERS, 64, 64), lambda i: (0, 0, 0))
    rows = pl.BlockSpec((step, 64, 256), lambda i: (i, 0, 0))
    return pl.pallas_call(
        finish,
        grid=(32 // step,),
        out_shape=[small, small, jax.ShapeDtypeStruct((64, 8192), F32)],
        in_specs=[whole, whole, pl.BlockSpec((2, 64, 64), lambda i: (0, 0, 0)), rows, rows],
        out_specs=[whole, whole, pl.BlockSpec((64, step * 256), lambda i: (0, i))],
    )(alphas, betas, factors, last_rows, old_rows)


def solution(mesh):
    in_specs = (
        P(None, "row"),
        P("row", "col", None, None, None),
        P("row", "col", None),
        P("row", "col", None),
    )
    out_specs = (P(), P(), P(None, "row"))
    return jax.shard_map(shards, mesh=mesh, in_specs=in_specs, out_specs=out_specs, check_vma=False)
```
